128 devices in a mesh: ta: 2 (over x_hi), ha: 8 (over y, x_lo), wa: 8 (over z, core).
Axes of the slice: x: 4 (x_hi: 2, x_lo: 2; x = x_hi * 2 + x_lo), y: 4, z: 4, core: 2. Of those that a mesh axis runs over, the one named last changes fastest.
Arguments:
- tokens: bfloat16 [8, 56, 56, 384], P('ta', 'ha', 'wa'), may hold values from -6 to 6
- upstream: bfloat16 [8, 56, 56, 384], P('ta', 'ha', 'wa'), may hold values from -6 to 6
- qkv_one: bfloat16 [384, 1152], replicated, may hold values from -0.3125 to 0.3125
- proj_one: bfloat16 [384, 384], replicated, may hold values from -0.3125 to 0.3125
- table_one: float32 [12, 1183], replicated, may hold values from -4 to 320
- expand_one: bfloat16 [384, 1536], replicated, may hold values from -0.3125 to 0.3125
- contract_one: bfloat16 [1536, 384], replicated, may hold values from -0.15625 to 0.15625
- qkv_two: bfloat16 [384, 1152], replicated, may hold values from -0.3125 to 0.3125
- proj_two: bfloat16 [384, 384], replicated, may hold values from -0.3125 to 0.3125
- table_two: float32 [12, 1183], replicated, may hold values from -4 to 320
- expand_two: bfloat16 [384, 1536], replicated, may hold values from -0.3125 to 0.3125
- contract_two: bfloat16 [1536, 384], replicated, may hold values from -0.15625 to 0.15625
Outputs:
- grad_tokens: bfloat16 [8, 56, 56, 384], P('ta', 'ha', 'wa')
- grad_qkv_one: float32 [384, 1152], P(('ta', 'ha', 'wa'))
- grad_proj_one: float32 [384, 384], P(('ta', 'ha', 'wa'))
- grad_table_one: float32 [12, 1183], replicated
- grad_expand_one: float32 [384, 1536], P(('ta', 'ha', 'wa'))
- grad_contract_one: float32 [1536, 384], P(('ta', 'ha', 'wa'))
- grad_qkv_two: float32 [384, 1152], P(('ta', 'ha', 'wa'))
- grad_proj_two: float32 [384, 384], P(('ta', 'ha', 'wa'))
- grad_table_two: float32 [12, 1183], replicated
- grad_expand_two: float32 [384, 1536], P(('ta', 'ha', 'wa'))
- grad_contract_two: float32 [1536, 384], P(('ta', 'ha', 'wa'))
The draws below stay inside these ranges and needn't reach their ends.
All inputs are finite; a program needn't handle non-finite values.
Results may differ from the reference program's by a relative error of at most 0.04.
Values may be sent and summed in bfloat16 or wider, within the bound.
No kernel may reach another device: no remote copies, remote signals or barrier semaphores. Data moves between devices by JAX's collectives and lax.ppermute only.
A program may use at most 256 MiB of HBM per device.

```python
import jax
import jax.numpy as jnp
from jax import lax

D = 384
HEADS = 12
FF = 1536
WT = 4
WH = 7
WW = 7
TABLE = 1183
NT = 8
NH = 56
NW = 56


def draw_table_one(key, part):
    key = jax.random.fold_in(key, 11)
    first_key = jax.random.fold_in(key, 0)
    return jnp.clip(jax.random.normal(first_key, (HEADS, TABLE), jnp.float32), -4.0, 4.0)


def draw_table_two(key, part):
    key = jax.random.fold_in(key, 12)
    first_key = jax.random.fold_in(key, 0)
    return jnp.clip(jax.random.normal(first_key, (HEADS, TABLE), jnp.float32), -4.0, 4.0)


def block_scale(own_key, shape, shards, least, high):
    level = 1.0
    for dim, shards_of in shards:
        steps = jax.random.uniform(jax.random.fold_in(jax.random.fold_in(own_key, 6), dim), (shards_of,), jnp.float32, least / len(shards), high / len(shards))
        level = level * jnp.repeat(jnp.exp(steps), shape[dim] // shards_of).reshape((-1,) + (1,) * (len(shape) - 1 - dim))
    return level


def normal_values(rng, dims, scale, most, shards=(), held_as=jnp.bfloat16):
    values = scale * jax.random.normal(rng, dims, jnp.float32)
    if shards:
        values = values * block_scale(rng, dims, shards, -0.22, 0.18)
    return jnp.clip(values, -most, most).astype(held_as)


def setup_inputs(seed: int = 0) -> dict:
    keys = jax.random.split(jax.random.key(seed), 13)
    return {
        "tokens": normal_values(keys[0], (NT, NH, NW, D), 1.0, 6.0, ((0, 2), (1, 8), (2, 8))),
        "upstream": normal_values(keys[1], (NT, NH, NW, D), 1.0, 6.0, ((0, 2), (1, 8), (2, 8))),
        "qkv_one": normal_values(keys[2], (D, 3 * D), D ** -0.5, 0.3125),
        "proj_one": normal_values(keys[3], (D, D), D ** -0.5, 0.3125),
        "table_one": draw_table_one(jax.random.fold_in(keys[12], 71), 0),
        "expand_one": normal_values(keys[5], (D, FF), D ** -0.5, 0.3125),
        "contract_one": normal_values(keys[6], (FF, D), FF ** -0.5, 0.15625),
        "qkv_two": normal_values(keys[7], (D, 3 * D), D ** -0.5, 0.3125),
        "proj_two": normal_values(keys[8], (D, D), D ** -0.5, 0.3125),
        "table_two": draw_table_two(jax.random.fold_in(keys[12], 71), 0),
        "expand_two": normal_values(keys[10], (D, FF), D ** -0.5, 0.3125),
        "contract_two": normal_values(keys[11], (FF, D), FF ** -0.5, 0.15625),
    }


epsilon = 1e-05

def layer_norm(values_in):
    widened = values_in.astype(jnp.float32)
    average = lax.optimization_barrier(jnp.mean(widened, axis=-1, keepdims=True))
    centred = widened - average
    spread = lax.optimization_barrier(jnp.mean(centred * centred, axis=-1, keepdims=True))
    return (centred * lax.rsqrt(spread + epsilon)).astype(jnp.bfloat16)

def relative_index():
    position = jnp.arange(WT * WH * WW, dtype=jnp.int32)
    along_t = position // (WH * WW)
    along_h = position // WW % WH
    along_w = position % WW
    delta_t = along_t[:, None] - along_t[None, :] + (WT - 1)
    delta_h = along_h[:, None] - along_h[None, :] + (WH - 1)
    delta_w = along_w[:, None] - along_w[None, :] + (WW - 1)
    return ((delta_t * (2 * WH - 1) + delta_h) * (2 * WW - 1) + delta_w).astype(jnp.int32)

def into_windows(grid):
    frames, height, width, depth = grid.shape
    blocks = grid.reshape(frames // WT, WT, height // WH, WH, width // WW, WW, depth)
    return blocks.transpose(0, 2, 4, 1, 3, 5, 6).reshape(-1, WT * WH * WW, depth)

def from_windows(windows, grid_shape):
    frames, height, width, depth = grid_shape
    blocks = windows.reshape(frames // WT, height // WH, width // WW, WT, WH, WW, depth)
    return blocks.transpose(0, 3, 1, 4, 2, 5, 6).reshape(grid_shape)

def window_attention(windows, weight_qkv, weight_proj, table, probe_qkv, probe_proj):
    window_count, length, depth = windows.shape
    head_size = depth // HEADS
    flat_rows = windows.reshape(window_count * length, depth)
    projected = (jnp.dot(flat_rows, weight_qkv, preferred_element_type=jnp.float32) + probe_qkv).astype(jnp.bfloat16)
    projected = projected.reshape(window_count, length, 3, HEADS, head_size)
    queries = projected[:, :, 0]
    keys_all = projected[:, :, 1]
    values_all = projected[:, :, 2]
    position_bias = jnp.take(table, relative_index(), axis=1)
    scores = jnp.einsum('blhe,bmhe->bhlm', queries, keys_all, preferred_element_type=jnp.float32) * head_size ** (-0.5)
    scores = scores + position_bias[None]
    weights_soft = jax.nn.softmax(scores, axis=-1).astype(jnp.bfloat16)
    context = jnp.einsum('bhlm,bmhe->blhe', weights_soft, values_all, preferred_element_type=jnp.float32).astype(jnp.bfloat16)
    context = context.reshape(window_count * length, depth)
    result = (jnp.dot(context, weight_proj, preferred_element_type=jnp.float32) + probe_proj).astype(jnp.bfloat16)
    return (result.reshape(window_count, length, depth), (flat_rows, context))

def feed_forward(hidden_in, weight_expand, weight_contract, probe_expand, probe_contract):
    normed = layer_norm(hidden_in).reshape(-1, hidden_in.shape[-1])
    expanded = jnp.dot(normed, weight_expand, preferred_element_type=jnp.float32) + probe_expand
    activated = jax.nn.gelu(expanded, approximate=False).astype(jnp.bfloat16)
    contracted = jnp.dot(activated, weight_contract, preferred_element_type=jnp.float32) + probe_contract
    result = (hidden_in.astype(jnp.float32) + contracted.reshape(hidden_in.shape)).astype(jnp.bfloat16)
    return (result, (normed, activated))

def outer_sum(stored, cotangent):
    return lax.dot_general(stored, cotangent.astype(jnp.bfloat16), (((0,), (0,)), ((), ())), preferred_element_type=jnp.float32)

def attention_grid(grid, weight_qkv, weight_proj, table, probe_qkv, probe_proj):
    windows = into_windows(grid)
    window_count, length, depth = windows.shape
    groups = window_count // 8

    def one_group(packed):
        return window_attention(packed[0], weight_qkv, weight_proj, table, packed[1], packed[2])
    results, (flat_rows, context) = lax.map(jax.checkpoint(one_group), (windows.reshape(groups, 8, length, depth), probe_qkv.reshape(groups, 8 * length, 3 * depth), probe_proj.reshape(groups, 8 * length, depth)))
    return (from_windows(results.reshape(window_count, length, depth), grid.shape), flat_rows.reshape(-1, depth), context.reshape(-1, depth))

def reference(tokens, upstream, qkv_one, proj_one, table_one, expand_one, contract_one, qkv_two, proj_two, table_two, expand_two, contract_two):
    depth = tokens.shape[3]
    hidden_units = expand_one.shape[1]
    row_count = tokens.shape[0] * tokens.shape[1] * tokens.shape[2]

    def zeros_for(columns):
        return jnp.zeros((row_count, columns), jnp.float32)
    probes = (zeros_for(3 * depth), zeros_for(depth), zeros_for(hidden_units), zeros_for(depth), zeros_for(3 * depth), zeros_for(depth), zeros_for(hidden_units), zeros_for(depth))
    shifts = (WT // 2, WH // 2, WW // 2)
    back_shifts = (-(WT // 2), -(WH // 2), -(WW // 2))

    def forward(inputs, first_table, second_table, probe_set):
        attended, flat_one, context_one = attention_grid(layer_norm(inputs), qkv_one, proj_one, first_table, probe_set[0], probe_set[1])
        mixed = (inputs.astype(jnp.float32) + attended.astype(jnp.float32)).astype(jnp.bfloat16)
        after_one, (normed_one, active_one) = feed_forward(mixed, expand_one, contract_one, probe_set[2], probe_set[3])
        rolled = jnp.roll(layer_norm(after_one), back_shifts, axis=(0, 1, 2))
        attended_two, flat_two, context_two = attention_grid(rolled, qkv_two, proj_two, second_table, probe_set[4], probe_set[5])
        returned = jnp.roll(attended_two, shifts, axis=(0, 1, 2))
        mixed_two = (after_one.astype(jnp.float32) + returned.astype(jnp.float32)).astype(jnp.bfloat16)
        after_two, (normed_two, active_two) = feed_forward(mixed_two, expand_two, contract_two, probe_set[6], probe_set[7])
        return (after_two, (flat_one, context_one, normed_one, active_one, flat_two, context_two, normed_two, active_two))
    final_out, pullback, stored = jax.vjp(forward, tokens, table_one, table_two, probes, has_aux=True)
    grad_tokens, grad_table_one, grad_table_two, probe_grads = pullback(upstream)
    gradients = [outer_sum(stored[index], probe_grads[index]) for index in range(8)]
    return (grad_tokens, gradients[0], gradients[1], grad_table_one, gradients[2], gradients[3], gradients[4], gradients[5], grad_table_two, gradients[6], gradients[7])
```

```python
import jax
import jax.numpy as jnp
from jax import lax
from jax.experimental import pallas as pl
from jax.experimental.pallas import tpu as pltpu
from jax.sharding import PartitionSpec as P

HEADS = 12
WT = 4
WH = 7
WW = 7
PITCH = 8
ROWS = WT * WH * PITCH
D = 384
FF = 1536
HD = 32
TABLE = 1183
TPAD = 1280
UPAD = 768
STEP = 32
CHUNK = 112
epsilon = 1e-05
f32 = jnp.float32
bf16 = jnp.bfloat16
NN = ((1,), (0,))
NT = ((1,), (1,))
AXES = ("ta", "ha", "wa")


def dot(a, b, dims):
    return lax.dot_general(a, b, (dims, ((), ())), preferred_element_type=f32)


def call(kernel, outs, scratch, *args):
    return pl.pallas_call(
        kernel,
        out_shape=outs,
        in_specs=[pl.BlockSpec(memory_space=pltpu.VMEM)] * len(args),
        out_specs=[pl.BlockSpec(memory_space=pltpu.VMEM)] * len(outs),
        scratch_shapes=scratch,
        compiler_params=pltpu.CompilerParams(vmem_limit_bytes=48 * 1024 * 1024),
    )(*args)


def out(shape, dtype):
    return jax.ShapeDtypeStruct(shape, dtype)


def row_steps():
    return range(0, ROWS, STEP)


def standardized(x):
    average = jnp.sum(x, axis=-1, keepdims=True) * (1.0 / D)
    centred = x - average
    spread = jnp.sum(centred * centred, axis=-1, keepdims=True) * (1.0 / D)
    scale = lax.rsqrt(spread + epsilon)
    return centred * scale, scale


def norm_pull(x, grad):
    unit, scale = standardized(x)
    mean_grad = jnp.sum(grad, axis=-1, keepdims=True) * (1.0 / D)
    mean_both = jnp.sum(grad * unit, axis=-1, keepdims=True) * (1.0 / D)
    return scale * (grad - mean_grad - unit * mean_both)


def norm_into(src, dst):
    for i in row_steps():
        rows = pl.ds(i, STEP)
        dst[rows, :] = standardized(src[rows, :].astype(f32))[0].astype(bf16)


def split3(x):
    hi = x.astype(bf16)
    rest = x - hi.astype(f32)
    mid = rest.astype(bf16)
    return hi, mid, (rest - mid.astype(f32)).astype(bf16)


def spread_onehot():
    col = lax.broadcasted_iota(jnp.int32, (1, UPAD), 1)
    group = lax.shift_right_logical(col, 3)
    w = jnp.bitwise_and(col, 7)
    valid = (w < WW) & (group < 91)
    target = jnp.where(valid, group * 13 + w + 6, -1)
    row = lax.broadcasted_iota(jnp.int32, (TPAD, UPAD), 0)
    return jnp.where(row == target, 1.0, 0.0).astype(bf16)


def build_bias(table_ref, bias_ref):
    sheared = []
    for h in range(HEADS):
        line = jnp.broadcast_to(table_ref[h : h + 1, :], (8, TPAD))
        sheared.append(pltpu.roll(line, 0, 1, stride=1, stride_axis=0))
    sheared = jnp.concatenate(sheared, axis=0)
    onehot = spread_onehot()
    hi, mid, lo = split3(sheared)
    u = dot(hi, onehot, NN) + dot(mid, onehot, NN) + dot(lo, onehot, NN)
    sub = lax.broadcasted_iota(jnp.int32, u.shape, 0)
    u = jnp.where(jnp.bitwise_and(sub, 7) == 7, -1e30, u)
    for hj in range(WH):
        base = (6 - hj) * 8
        y = jnp.concatenate([u[:, dt * 104 + base : dt * 104 + base + 56] for dt in range(7)], axis=1)
        for tj in range(WT):
            z = y[:, (3 - tj) * 56 : (3 - tj) * 56 + ROWS]
            bias_ref[:, tj * 56 + hj * 8 : tj * 56 + hj * 8 + 8, :] = z.reshape(HEADS, 8, ROWS)


def bias_kernel(table_ref, bias_ref):
    build_bias(table_ref, bias_ref)


def table_pull(ds_ref):
    du = jnp.zeros((HEADS * 8, UPAD), f32)
    for hj in range(WH):
        dy = jnp.zeros((HEADS * 8, 392), f32)
        for tj in range(WT):
            z = ds_ref[:, tj * 56 + hj * 8 : tj * 56 + hj * 8 + 8, :].reshape(HEADS * 8, ROWS)
            parts = []
            if tj < 3:
                parts.append(jnp.zeros((HEADS * 8, (3 - tj) * 56), f32))
            parts.append(z)
            if tj > 0:
                parts.append(jnp.zeros((HEADS * 8, tj * 56), f32))
            dy = dy + (jnp.concatenate(parts, axis=1) if len(parts) > 1 else parts[0])
        parts = []
        at = 0
        for dt in range(7):
            start = dt * 104 + (6 - hj) * 8
            if start > at:
                parts.append(jnp.zeros((HEADS * 8, start - at), f32))
            parts.append(dy[:, dt * 56 : dt * 56 + 56])
            at = start + 56
        parts.append(jnp.zeros((HEADS * 8, UPAD - at), f32))
        du = du + jnp.concatenate(parts, axis=1)
    onehot = spread_onehot()
    hi = du.astype(bf16)
    lo = (du - hi.astype(f32)).astype(bf16)
    return dot(hi, onehot, NT) + dot(lo, onehot, NT)


def unsheared(sheared):
    sub = jnp.bitwise_and(lax.broadcasted_iota(jnp.int32, sheared.shape, 0), 7)
    total = jnp.zeros_like(sheared)
    for wj in range(WW):
        moved = pltpu.roll(sheared, TPAD - wj, 1) if wj else sheared
        total = jnp.where(sub == wj, moved, total)
    return [jnp.sum(total[8 * h : 8 * h + 8], axis=0, keepdims=True) for h in range(HEADS)]


def head_mask(hh):
    lane = lax.broadcasted_iota(jnp.int32, (1, 128), 1)
    return (lane >= hh * HD) & (lane < hh * HD + HD)


def masked(value, hh):
    return jnp.where(head_mask(hh), value, jnp.zeros_like(value))


def attention_forward(n_ref, wqkv_ref, bias_ref, qkv_ref, p_ref, ctxt_ref, ctx_ref):
    for c in range(3):
        cols = slice(c * D, c * D + D)
        qkv_ref[:, cols] = dot(n_ref[...], wqkv_ref[:, cols], NN).astype(bf16)
    for g in range(3):
        lanes = slice(g * 128, g * 128 + 128)
        q = qkv_ref[:, g * 128 : g * 128 + 128]
        k = qkv_ref[:, D + g * 128 : D + g * 128 + 128]
        v = qkv_ref[:, 2 * D + g * 128 : 2 * D + g * 128 + 128]
        vt = v.astype(f32).T.astype(bf16)
        for hh in range(4):
            h = 4 * g + hh
            s = dot(k, masked(q, hh), NT) * (HD**-0.5) + bias_ref[h]
            top = jnp.max(s, axis=0, keepdims=True)
            e = jnp.exp(s - top)
            p = (e * (1.0 / jnp.sum(e, axis=0, keepdims=True))).astype(bf16)
            p_ref[h] = p
            ctxt_ref[h * HD : h * HD + HD, :] = dot(vt[hh * HD : hh * HD + HD], p, NN)
        ctx_ref[:, lanes] = ctxt_ref[g * 128 : g * 128 + 128, :].T.astype(bf16)


def attention_backward(dctx, qkv_ref, p_ref, ds_ref, dqt_ref, dqkv_ref):
    for g in range(3):
        q = qkv_ref[:, g * 128 : g * 128 + 128]
        k = qkv_ref[:, D + g * 128 : D + g * 128 + 128]
        v = qkv_ref[:, 2 * D + g * 128 : 2 * D + g * 128 + 128]
        dc = dctx[:, g * 128 : g * 128 + 128]
        kt = k.astype(f32).T.astype(bf16)
        dk = jnp.zeros((ROWS, 128), f32)
        dv = jnp.zeros((ROWS, 128), f32)
        for hh in range(4):
            h = 4 * g + hh
            dch = masked(dc, hh)
            p = p_ref[h]
            p32 = p.astype(f32)
            dp = dot(v, dch, NT)
            delta = jnp.sum(p32 * dp, axis=0, keepdims=True)
            ds = p32 * (dp - delta)
            ds_ref[h] = ds.astype(ds_ref.dtype)
            dsb = ds.astype(bf16)
            dv = dv + dot(p, dch, NN)
            dk = dk + dot(dsb, masked(q, hh), NN)
            dqt_ref[h * HD : h * HD + HD, :] = dot(kt[hh * HD : hh * HD + HD], dsb, NN)
        dq = dqt_ref[g * 128 : g * 128 + 128, :].T
        dqkv_ref[:, g * 128 : g * 128 + 128] = (dq * (HD**-0.5)).astype(bf16)
        dqkv_ref[:, D + g * 128 : D + g * 128 + 128] = (dk * (HD**-0.5)).astype(bf16)
        dqkv_ref[:, 2 * D + g * 128 : 2 * D + g * 128 + 128] = dv.astype(bf16)


def expand_gelu(n2_ref, we_ref, e_ref, act_ref, slope_ref):
    for c in range(4):
        cols = slice(c * D, c * D + D)
        e_ref[...] = dot(n2_ref[...], we_ref[:, cols], NN)
        for i in row_steps():
            rows = slice(i, i + STEP)
            x = e_ref[rows, :]
            cdf = 0.5 + 0.5 * lax.erf(x * 0.7071067811865476)
            act_ref[rows, cols] = (x * cdf).astype(bf16)
            slope = cdf + x * (jnp.exp(x * x * -0.5) * 0.3989422804014327)
            slope_ref[rows, cols] = slope.astype(slope_ref.dtype)


def first_forward(
    x_ref, table_ref, wqkv_ref, wp_ref, we_ref, wc_ref,
    n1_ref, qkv_ref, p_ref, ctx_ref, h1_ref, n2_ref, act_ref, slope_ref, y_ref,
    bias_ref, ctxt_ref, big_ref,
):
    build_bias(table_ref, bias_ref)
    norm_into(x_ref, n1_ref)
    attention_forward(n1_ref, wqkv_ref, bias_ref, qkv_ref, p_ref, ctxt_ref, ctx_ref)
    big_ref[...] = dot(ctx_ref[...], wp_ref[...], NN)
    for i in row_steps():
        rows = slice(i, i + STEP)
        a = big_ref[rows, :].astype(bf16).astype(f32)
        h = (x_ref[rows, :].astype(f32) + a).astype(bf16)
        h1_ref[rows, :] = h
        n2_ref[rows, :] = standardized(h.astype(f32))[0].astype(bf16)
    expand_gelu(n2_ref, we_ref, big_ref, act_ref, slope_ref)
    big_ref[...] = dot(act_ref[...], wc_ref[...], NN)
    for i in row_steps():
        rows = slice(i, i + STEP)
        y_ref[rows, :] = (h1_ref[rows, :].astype(f32) + big_ref[rows, :]).astype(bf16)


def feed_backward(gy_ref, act_unused, slope_ref, h_ref, we_ref, wc_ref, de_ref, big_ref, dh_ref):
    for c in range(4):
        cols = slice(c * D, c * D + D)
        big_ref[...] = dot(gy_ref[...], wc_ref[cols, :], NT)
        for i in row_steps():
            rows = slice(i, i + STEP)
            da = big_ref[rows, :].astype(bf16).astype(f32)
            de_ref[rows, cols] = (da * slope_ref[rows, cols].astype(f32)).astype(bf16)
    big_ref[...] = dot(de_ref[...], we_ref[...], NT)
    for i in row_steps():
        rows = slice(i, i + STEP)
        g = big_ref[rows, :].astype(bf16).astype(f32)
        back = norm_pull(h_ref[rows, :].astype(f32), g).astype(bf16)
        dh_ref[rows, :] = (gy_ref[rows, :].astype(f32) + back.astype(f32)).astype(bf16)


def second_whole(
    y_ref, up_ref, bias_ref, wqkv_ref, wp_ref, we_ref, wc_ref,
    n1_ref, ctx_ref, n2_ref, act_ref, dqkv_ref, dh_ref, de_ref, ds_ref, gy_ref,
    qkv_ref, p_ref, ctxt_ref, h2_ref, slope_ref, dctx_ref, big_ref,
):
    norm_into(y_ref, n1_ref)
    attention_forward(n1_ref, wqkv_ref, bias_ref, qkv_ref, p_ref, ctxt_ref, ctx_ref)
    big_ref[...] = dot(ctx_ref[...], wp_ref[...], NN)
    for i in row_steps():
        rows = slice(i, i + STEP)
        a = big_ref[rows, :].astype(bf16).astype(f32)
        h = (y_ref[rows, :].astype(f32) + a).astype(bf16)
        h2_ref[rows, :] = h
        n2_ref[rows, :] = standardized(h.astype(f32))[0].astype(bf16)
    expand_gelu(n2_ref, we_ref, big_ref, act_ref, slope_ref)
    feed_backward(up_ref, act_ref, slope_ref, h2_ref, we_ref, wc_ref, de_ref, big_ref, dh_ref)
    dctx_ref[...] = dot(dh_ref[...], wp_ref[...], NT).astype(bf16)
    attention_backward(dctx_ref, qkv_ref, p_ref, ds_ref, ctxt_ref, dqkv_ref)
    attention_input_pull(y_ref, dqkv_ref, wqkv_ref, big_ref, dh_ref, gy_ref)


def attention_input_pull(x_ref, dqkv_ref, wqkv_ref, big_ref, dh_ref, dx_ref):
    big_ref[...] = dot(dqkv_ref[...], wqkv_ref[...], NT)
    for i in row_steps():
        rows = slice(i, i + STEP)
        g = big_ref[rows, :].astype(bf16).astype(f32)
        back = norm_pull(x_ref[rows, :].astype(f32), g).astype(bf16)
        dx_ref[rows, :] = (dh_ref[rows, :].astype(f32) + back.astype(f32)).astype(bf16)


def first_backward(
    gy_ref, x_ref, qkv_ref, p_ref, h1_ref, slope_ref, wqkv_ref, wp_ref, we_ref, wc_ref,
    dqkv_ref, dh_ref, de_ref, ds_ref, dx_ref,
    dqt_ref, dctx_ref, big_ref,
):
    feed_backward(gy_ref, None, slope_ref, h1_ref, we_ref, wc_ref, de_ref, big_ref, dh_ref)
    dctx_ref[...] = dot(dh_ref[...], wp_ref[...], NT).astype(bf16)
    attention_backward(dctx_ref, qkv_ref, p_ref, ds_ref, dqt_ref, dqkv_ref)
    attention_input_pull(x_ref, dqkv_ref, wqkv_ref, big_ref, dh_ref, dx_ref)


def picker(columns, per):
    row = lax.broadcasted_iota(jnp.int32, (128, columns), 0)
    col = lax.broadcasted_iota(jnp.int32, (128, columns), 1)
    return [jnp.where(col == row * per + r, 1.0, 0.0).astype(bf16) for r in range(per)]


def weights_kernel(
    n1_ref, ctx_ref, n2_ref, act_ref, dqkv_ref, da_ref, de_ref, gy_ref, ds_ref,
    out_ref, f_ref,
):
    pick3 = picker(D, 3)

    def place(first, x_ref, g_ref, picks):
        width = g_ref.shape[1] // 128
        for r, pick in enumerate(picks):
            xt = dot(pick, x_ref[...], NT).astype(bf16)
            dw = dot(xt, g_ref[...], NN)
            for c in range(width):
                f_ref[pl.ds(first + r * width + c, 128, stride=CHUNK), :] = dw[:, c * 128 : c * 128 + 128]

    place(0, n1_ref, dqkv_ref, pick3)
    place(27, ctx_ref, da_ref, pick3)
    place(36, n2_ref, de_ref, pick3)
    place(72, act_ref, gy_ref, picker(FF, 12))
    lines = unsheared(table_pull(ds_ref))
    zero = jnp.zeros((128, 128), f32)
    for j in range(108, CHUNK):
        f_ref[pl.ds(j, 128, stride=CHUNK), :] = zero
    for h in range(HEADS):
        for c in range(10):
            at = (h * 10 + c) * CHUNK + 108
            f_ref[at : at + 1, :] = lines[h][:, c * 128 : c * 128 + 128]

    def step(i, carry):
        rows = pl.ds(pl.multiple_of(i * 256, 256), 256)
        out_ref[rows, :] = f_ref[rows, :].astype(bf16)
        return carry

    lax.fori_loop(0, 128 * CHUNK // 256, step, 0)


def run_bias(table):
    return call(bias_kernel, [out((HEADS, ROWS, ROWS), f32)], [], table)[0]


def rows(width, dtype=bf16):
    return out((ROWS, width), dtype)


def scr(shape, dtype):
    return pltpu.VMEM(shape, dtype)


def run_first_forward(x, table, wqkv, wp, we, wc):
    return call(
        first_forward,
        [rows(D), rows(3 * D), out((HEADS, ROWS, ROWS), bf16), rows(D), rows(D), rows(D), rows(FF), rows(FF), rows(D)],
        [scr((HEADS, ROWS, ROWS), f32), scr((D, ROWS), f32), scr((ROWS, D), f32)],
        x, table, wqkv, wp, we, wc,
    )


def run_second(y, up, bias, wqkv, wp, we, wc):
    return call(
        second_whole,
        [rows(D), rows(D), rows(D), rows(FF), rows(3 * D), rows(D), rows(FF), out((HEADS, ROWS, ROWS), f32), rows(D)],
        [
            scr((ROWS, 3 * D), bf16), scr((HEADS, ROWS, ROWS), bf16), scr((D, ROWS), f32), scr((ROWS, D), bf16),
            scr((ROWS, FF), bf16), scr((ROWS, D), bf16), scr((ROWS, D), f32),
        ],
        y, up, bias, wqkv, wp, we, wc,
    )


def run_first_backward(gy, x, qkv, p, h1, slope, wqkv, wp, we, wc):
    return call(
        first_backward,
        [rows(3 * D), rows(D), rows(FF), out((HEADS, ROWS, ROWS), f32), rows(D)],
        [scr((D, ROWS), f32), scr((ROWS, D), bf16), scr((ROWS, D), f32)],
        gy, x, qkv, p, h1, slope, wqkv, wp, we, wc,
    )


def run_weights(n1, ctx, n2, act, dqkv, da, de, gy, ds):
    return call(
        weights_kernel, [out((128 * CHUNK, 128), bf16)], [scr((128 * CHUNK, 128), f32)],
        n1, ctx, n2, act, dqkv, da, de, gy, ds,
    )[0]


def passed_along(block, axis, distance):
    devices = range(lax.axis_size(axis))
    route = [((i - distance) % len(devices), i) for i in devices]
    return lax.ppermute(block, axis, route)


def edge_of(grid, dim, width, direction):
    extent = grid.shape[dim]
    if direction < 0:
        return lax.slice_in_dim(grid, 0, width, axis=dim)
    return lax.slice_in_dim(grid, extent - width, extent, axis=dim)


def rejoin(grid, dim, width, direction, arrived):
    extent = grid.shape[dim]
    if direction < 0:
        return jnp.concatenate([lax.slice_in_dim(grid, width, extent, axis=dim), arrived], axis=dim)
    return jnp.concatenate([arrived, lax.slice_in_dim(grid, 0, extent - width, axis=dim)], axis=dim)


def roll_grid(grid, direction):
    for dim, (axis, width) in enumerate(zip(AXES, (WT // 2, WH // 2, WW // 2))):
        moved = passed_along(edge_of(grid, dim, width, direction), axis, direction)
        grid = rejoin(grid, dim, width, direction, moved)
    return grid


def to_rows(grid):
    return jnp.pad(grid, ((0, 0), (0, 0), (0, 1), (0, 0))).reshape(ROWS, D)


def to_grid(flat):
    return flat.reshape(WT, WH, PITCH, D)[:, :, :WW]


def scattered(buffer):
    spread = lax.all_to_all(buffer.reshape(128, CHUNK, 128), AXES, 0, 0, tiled=True)
    return jnp.sum(spread.astype(f32), axis=0)


def weight_parts(chunk):
    return (
        chunk[0:27].reshape(3, 3 * D),
        chunk[27:36].reshape(3, D),
        chunk[36:72].reshape(3, FF),
        chunk[72:108].reshape(12, D),
    )


def body(
    tokens, upstream, qkv_one, proj_one, table_one, expand_one, contract_one,
    qkv_two, proj_two, table_two, expand_two, contract_two,
):
    def padded(table):
        return jnp.pad(table, ((0, 16 - HEADS), (0, TPAD - TABLE)))

    x = to_rows(tokens)
    n1, qkv, p, ctx, h1, n2, act, slope, y = run_first_forward(
        x, padded(table_one), qkv_one, proj_one, expand_one, contract_one
    )
    bias = run_bias(padded(table_two))
    up = to_rows(roll_grid(upstream, -1))
    rolled = to_rows(roll_grid(to_grid(y), -1))
    n1b, ctxb, n2b, actb, dqkvb, dhb, deb, dsb, gyb = run_second(
        rolled, up, bias, qkv_two, proj_two, expand_two, contract_two
    )
    gy = to_rows(roll_grid(to_grid(gyb), 1))
    second = scattered(run_weights(n1b, ctxb, n2b, actb, dqkvb, dhb, deb, up, dsb))
    dqkv, dh, de, ds, dx = run_first_backward(
        gy, x, qkv, p, h1, slope, qkv_one, proj_one, expand_one, contract_one
    )
    first = scattered(run_weights(n1, ctx, n2, act, dqkv, dh, de, gy, ds))
    lines = jnp.concatenate([first[108:109], second[108:109]], axis=0)
    tables = lax.all_to_all(jnp.broadcast_to(lines[None], (128, 2, 128)), AXES, 0, 0, tiled=True)

    def table_of(which):
        return tables[:120, which].reshape(HEADS, TPAD)[:, :TABLE]

    g1, g2 = weight_parts(first), weight_parts(second)
    return (
        to_grid(dx), g1[0], g1[1], table_of(0), g1[2], g1[3],
        g2[0], g2[1], table_of(1), g2[2], g2[3],
    )


def solution(mesh):
    grid = P("ta", "ha", "wa", None)
    rows_split = P(AXES, None)
    return jax.shard_map(
        body,
        mesh=mesh,
        in_specs=(grid, grid) + (P(),) * 10,
        out_specs=(
            grid, rows_split, rows_split, P(), rows_split, rows_split,
            rows_split, rows_split, P(), rows_split, rows_split,
        ),
        check_vma=False,
    )
```

```python
import jax
import jax.numpy as jnp
from jax import lax
from jax.experimental import pallas as pl
from jax.experimental.pallas import tpu as pltpu
from jax.sharding import PartitionSpec as P

HEADS = 12
WT = 4
WH = 7
WW = 7
PITCH = 8
ROWS = WT * WH * PITCH
D = 384
FF = 1536
HD = 32
TABLE = 1183
TPAD = 1280
UPAD = 768
STEP = 32
CHUNK = 112
VMEM_LIMIT = 32 * 1024 * 1024
epsilon = 1e-05
f32 = jnp.float32
bf16 = jnp.bfloat16
NN = ((1,), (0,))
NT = ((1,), (1,))
AXES = ("ta", "ha", "wa")


def dot(a, b, dims):
    return lax.dot_general(a, b, (dims, ((), ())), preferred_element_type=f32)


class Held:
    def __init__(self, refs, incoming, outgoing):
        self.__dict__.update(refs)
        self.incoming = dict(incoming)
        self.outgoing = dict(outgoing)

    def need(self, *names):
        for name in names:
            if name in self.incoming:
                self.incoming.pop(name).wait()

    def ready(self, *names):
        for name in names:
            if name in self.outgoing:
                self.outgoing.pop(name).start()


def launch(kernel, ins, outs, scratch=()):
    places = {"far": pltpu.HBM, "near": pltpu.VMEM, "flag": pltpu.SMEM}
    far_ins = [n for n, (_, space) in ins.items() if space == "far"]
    far_outs = [n for n, (_, _, space) in outs.items() if space == "far"]
    scratch = dict(scratch)
    buffers = {n: pltpu.VMEM(ins[n][0].shape, ins[n][0].dtype) for n in far_ins}
    buffers.update({n: pltpu.VMEM(outs[n][0], outs[n][1]) for n in far_outs})

    def wrapped(*refs):
        named = dict(zip(list(ins) + list(outs), refs))
        rest = refs[len(named) :]
        near = dict(zip(list(scratch) + list(buffers), rest))
        sems = rest[-1]
        incoming, outgoing = {}, {}
        for i, n in enumerate(far_ins):
            incoming[n] = pltpu.make_async_copy(named[n], near[n], sems.at[i])
            incoming[n].start()
        for i, n in enumerate(far_outs):
            outgoing[n] = pltpu.make_async_copy(near[n], named[n], sems.at[len(far_ins) + i])
        kernel(Held({**named, **near}, incoming, outgoing))
        for n in far_outs:
            outgoing[n].wait()

    results = pl.pallas_call(
        wrapped,
        out_shape=[
            pltpu.HBM(shape, dtype) if space == "far" else jax.ShapeDtypeStruct(shape, dtype)
            for shape, dtype, space in outs.values()
        ],
        in_specs=[pl.BlockSpec(memory_space=places[space]) for _, space in ins.values()],
        out_specs=[pl.BlockSpec(memory_space=places[space]) for _, _, space in outs.values()],
        scratch_shapes=list(scratch.values())
        + list(buffers.values())
        + [pltpu.SemaphoreType.DMA((max(1, len(far_ins) + len(far_outs)),))],
        compiler_params=pltpu.CompilerParams(vmem_limit_bytes=VMEM_LIMIT),
    )(
        *[
            pltpu.with_memory_space_constraint(array, pltpu.HBM) if space == "far" else array
            for array, space in ins.values()
        ]
    )
    return dict(zip(outs, results))


def row_steps():
    return range(0, ROWS, STEP)


def standardized(x):
    average = jnp.sum(x, axis=-1, keepdims=True) * (1.0 / D)
    centred = x - average
    spread = jnp.sum(centred * centred, axis=-1, keepdims=True) * (1.0 / D)
    scale = lax.rsqrt(spread + epsilon)
    return centred * scale, scale


def norm_pull(x, grad):
    unit, scale = standardized(x)
    mean_grad = jnp.sum(grad, axis=-1, keepdims=True) * (1.0 / D)
    mean_both = jnp.sum(grad * unit, axis=-1, keepdims=True) * (1.0 / D)
    return scale * (grad - mean_grad - unit * mean_both)


def norm_into(src, dst):
    for i in row_steps():
        rows = pl.ds(i, STEP)
        dst[rows, :] = standardized(src[rows, :].astype(f32))[0].astype(bf16)


def split3(x):
    hi = x.astype(bf16)
    rest = x - hi.astype(f32)
    mid = rest.astype(bf16)
    return hi, mid, (rest - mid.astype(f32)).astype(bf16)


def spread_onehot():
    col = lax.broadcasted_iota(jnp.int32, (1, UPAD), 1)
    group = lax.shift_right_logical(col, 3)
    w = jnp.bitwise_and(col, 7)
    valid = (w < WW) & (group < 91)
    target = jnp.where(valid, group * 13 + w + 6, -1)
    row = lax.broadcasted_iota(jnp.int32, (TPAD, UPAD), 0)
    return jnp.where(row == target, 1.0, 0.0).astype(bf16)


def build_bias(table_ref, bias_ref, wide_ref):
    wide_ref[...] = jnp.zeros_like(wide_ref)
    wide_ref[:HEADS, :TABLE] = table_ref[...]
    sheared = []
    for h in range(HEADS):
        line = jnp.broadcast_to(wide_ref[h : h + 1, :], (8, TPAD))
        sheared.append(pltpu.roll(line, 0, 1, stride=1, stride_axis=0))
    sheared = jnp.concatenate(sheared, axis=0)
    onehot = spread_onehot()
    hi, mid, lo = split3(sheared)
    u = dot(hi, onehot, NN) + dot(mid, onehot, NN) + dot(lo, onehot, NN)
    sub = lax.broadcasted_iota(jnp.int32, u.shape, 0)
    u = jnp.where(jnp.bitwise_and(sub, 7) == 7, -1e30, u)
    for hj in range(WH):
        base = (6 - hj) * 8
        y = jnp.concatenate([u[:, dt * 104 + base : dt * 104 + base + 56] for dt in range(7)], axis=1)
        for tj in range(WT):
            z = y[:, (3 - tj) * 56 : (3 - tj) * 56 + ROWS]
            bias_ref[:, tj * 56 + hj * 8 : tj * 56 + hj * 8 + 8, :] = z.reshape(HEADS, 8, ROWS)


def table_pull(ds_ref):
    du = jnp.zeros((HEADS * 8, UPAD), f32)
    for hj in range(WH):
        dy = jnp.zeros((HEADS * 8, 392), f32)
        for tj in range(WT):
            z = ds_ref[:, tj * 56 + hj * 8 : tj * 56 + hj * 8 + 8, :].astype(f32).reshape(HEADS * 8, ROWS)
            parts = []
            if tj < 3:
                parts.append(jnp.zeros((HEADS * 8, (3 - tj) * 56), f32))
            parts.append(z)
            if tj > 0:
                parts.append(jnp.zeros((HEADS * 8, tj * 56), f32))
            dy = dy + (jnp.concatenate(parts, axis=1) if len(parts) > 1 else parts[0])
        parts = []
        at = 0
        for dt in range(7):
            start = dt * 104 + (6 - hj) * 8
            if start > at:
                parts.append(jnp.zeros((HEADS * 8, start - at), f32))
            parts.append(dy[:, dt * 56 : dt * 56 + 56])
            at = start + 56
        parts.append(jnp.zeros((HEADS * 8, UPAD - at), f32))
        du = du + jnp.concatenate(parts, axis=1)
    onehot = spread_onehot()
    hi = du.astype(bf16)
    lo = (du - hi.astype(f32)).astype(bf16)
    return dot(hi, onehot, NT) + dot(lo, onehot, NT)


def unsheared(sheared):
    sub = jnp.bitwise_and(lax.broadcasted_iota(jnp.int32, sheared.shape, 0), 7)
    total = jnp.zeros_like(sheared)
    for wj in range(WW):
        moved = pltpu.roll(sheared, TPAD - wj, 1) if wj else sheared
        total = jnp.where(sub == wj, moved, total)
    return [jnp.sum(total[8 * h : 8 * h + 8], axis=0, keepdims=True) for h in range(HEADS)]


def head_mask(hh):
    lane = lax.broadcasted_iota(jnp.int32, (1, 128), 1)
    return (lane >= hh * HD) & (lane < hh * HD + HD)


def masked(value, hh):
    return jnp.where(head_mask(hh), value, jnp.zeros_like(value))


def attention_forward(n_ref, wqkv_ref, bias_ref, qkv_ref, p_ref, ctxt_ref, ctx_ref):
    for c in range(3):
        cols = slice(c * D, c * D + D)
        qkv_ref[:, cols] = dot(n_ref[...], wqkv_ref[:, cols], NN).astype(bf16)
    for g in range(3):
        lanes = slice(g * 128, g * 128 + 128)
        q = qkv_ref[:, g * 128 : g * 128 + 128]
        k = qkv_ref[:, D + g * 128 : D + g * 128 + 128]
        v = qkv_ref[:, 2 * D + g * 128 : 2 * D + g * 128 + 128]
        vt = v.astype(f32).T.astype(bf16)
        for hh in range(4):
            h = 4 * g + hh
            s = dot(k, masked(q, hh), NT) * (HD**-0.5) + bias_ref[h]
            top = jnp.max(s, axis=0, keepdims=True)
            e = jnp.exp(s - top)
            p = (e * (1.0 / jnp.sum(e, axis=0, keepdims=True))).astype(bf16)
            p_ref[h] = p
            ctxt_ref[h * HD : h * HD + HD, :] = dot(vt[hh * HD : hh * HD + HD], p, NN)
        ctx_ref[:, lanes] = ctxt_ref[g * 128 : g * 128 + 128, :].T.astype(bf16)


def attention_backward(dctx, qkv_ref, p_ref, ds_ref, dqt_ref, dqkv_ref):
    for g in range(3):
        q = qkv_ref[:, g * 128 : g * 128 + 128]
        k = qkv_ref[:, D + g * 128 : D + g * 128 + 128]
        v = qkv_ref[:, 2 * D + g * 128 : 2 * D + g * 128 + 128]
        dc = dctx[:, g * 128 : g * 128 + 128]
        kt = k.astype(f32).T.astype(bf16)
        dk = jnp.zeros((ROWS, 128), f32)
        dv = jnp.zeros((ROWS, 128), f32)
        for hh in range(4):
            h = 4 * g + hh
            dch = masked(dc, hh)
            p = p_ref[h]
            p32 = p.astype(f32)
            dp = dot(v, dch, NT)
            delta = jnp.sum(p32 * dp, axis=0, keepdims=True)
            ds = p32 * (dp - delta)
            ds_ref[h] = ds.astype(ds_ref.dtype)
            dsb = ds.astype(bf16)
            dv = dv + dot(p, dch, NN)
            dk = dk + dot(dsb, masked(q, hh), NN)
            dqt_ref[h * HD : h * HD + HD, :] = dot(kt[hh * HD : hh * HD + HD], dsb, NN)
        dq = dqt_ref[g * 128 : g * 128 + 128, :].T
        dqkv_ref[:, g * 128 : g * 128 + 128] = (dq * (HD**-0.5)).astype(bf16)
        dqkv_ref[:, D + g * 128 : D + g * 128 + 128] = (dk * (HD**-0.5)).astype(bf16)
        dqkv_ref[:, 2 * D + g * 128 : 2 * D + g * 128 + 128] = dv.astype(bf16)


def expand_gelu(n2_ref, we_ref, e_ref, act_ref, slope_ref):
    for c in range(4):
        cols = slice(c * D, c * D + D)
        e_ref[...] = dot(n2_ref[...], we_ref[:, cols], NN)
        for i in row_steps():
            rows = slice(i, i + STEP)
            x = e_ref[rows, :]
            cdf = 0.5 + 0.5 * lax.erf(x * 0.7071067811865476)
            act_ref[rows, cols] = (x * cdf).astype(bf16)
            slope = cdf + x * (jnp.exp(x * x * -0.5) * 0.3989422804014327)
            slope_ref[rows, cols] = slope.astype(slope_ref.dtype)


def attention_and_feed(m, x):
    m.need("wqkv")
    build_bias(m.table, m.bias, m.wide)
    norm_into(x, m.n1)
    attention_forward(m.n1, m.wqkv, m.bias, m.qkv, m.p, m.turned, m.ctx)
    m.need("wp", "we", "wc")
    m.ready("n1", "qkv", "p", "ctx")
    m.big[...] = dot(m.ctx[...], m.wp[...], NN)
    for i in row_steps():
        rows = slice(i, i + STEP)
        a = m.big[rows, :].astype(bf16).astype(f32)
        h = (x[rows, :].astype(f32) + a).astype(bf16)
        m.h[rows, :] = h
        m.n2[rows, :] = standardized(h.astype(f32))[0].astype(bf16)
    expand_gelu(m.n2, m.we, m.big, m.act, m.slope)
    m.ready("h", "n2", "act", "slope")


def first_forward(m):
    attention_and_feed(m, m.x)
    m.big[...] = dot(m.act[...], m.wc[...], NN)
    for i in row_steps():
        rows = slice(i, i + STEP)
        m.y[rows, :] = (m.h[rows, :].astype(f32) + m.big[rows, :]).astype(bf16)


def feed_backward(gy_ref, slope_ref, h_ref, we_ref, wc_ref, de_ref, big_ref, dh_ref):
    for c in range(4):
        cols = slice(c * D, c * D + D)
        big_ref[...] = dot(gy_ref[...], wc_ref[cols, :], NT)
        for i in row_steps():
            rows = slice(i, i + STEP)
            da = big_ref[rows, :].astype(bf16).astype(f32)
            de_ref[rows, cols] = (da * slope_ref[rows, cols].astype(f32)).astype(bf16)
    big_ref[...] = dot(de_ref[...], we_ref[...], NT)
    for i in row_steps():
        rows = slice(i, i + STEP)
        g = big_ref[rows, :].astype(bf16).astype(f32)
        back = norm_pull(h_ref[rows, :].astype(f32), g).astype(bf16)
        dh_ref[rows, :] = (gy_ref[rows, :].astype(f32) + back.astype(f32)).astype(bf16)


def attention_input_pull(x_ref, dqkv_ref, wqkv_ref, big_ref, dh_ref, dx_ref):
    big_ref[...] = dot(dqkv_ref[...], wqkv_ref[...], NT)
    for i in row_steps():
        rows = slice(i, i + STEP)
        g = big_ref[rows, :].astype(bf16).astype(f32)
        back = norm_pull(x_ref[rows, :].astype(f32), g).astype(bf16)
        dx_ref[rows, :] = (dh_ref[rows, :].astype(f32) + back.astype(f32)).astype(bf16)


def backward(m, x, gy, dx):
    m.need("wc", "slope", "we", "h")
    feed_backward(gy, m.slope, m.h, m.we, m.wc, m.de, m.big, m.dh)
    m.need("wp", "qkv", "p", "wqkv")
    m.dctx[...] = dot(m.dh[...], m.wp[...], NT).astype(bf16)
    attention_backward(m.dctx, m.qkv, m.p, m.ds, m.turned, m.dqkv)
    attention_input_pull(x, m.dqkv, m.wqkv, m.big, m.dh, dx)
    m.ready("ds", "dqkv", "de", "dh")


def second_whole(m):
    attention_and_feed(m, m.y)
    backward(m, m.y, m.up, m.gy)


def first_backward(m):
    backward(m, m.x, m.gy, m.dx)
    m.need("n1", "ctx", "n2", "act")
    weight_sums(m)


def picker(per):
    count = D // per
    row = lax.broadcasted_iota(jnp.int32, (D, 1), 0)
    r = jnp.zeros((D, 1), jnp.int32)
    for step in range(1, per):
        r = r + jnp.where(row >= step * count, 1, 0)
    target = (row - r * count) * per + r
    col = lax.broadcasted_iota(jnp.int32, (D, D), 1)
    return jnp.where(col == target, 1.0, 0.0).astype(bf16)


def weights_kernel(m):
    m.passed[...] = m.carried[...]
    m.need("n1", "dqkv", "ctx", "dh", "n2", "de", "act", "ds")
    weight_sums(m)


def weight_sums(m):
    f_ref = m.f
    pick = picker(3)

    def place(first, x, g_ref, pick, per, owner):
        width = g_ref.shape[1] // 128
        count = D // per
        xt = dot(pick, x, NT).astype(bf16)
        for c in range(0, width, 3):
            dw = dot(xt, g_ref[:, c * 128 : c * 128 + 384], NN)
            for r in range(per):
                for k in range(3):
                    at = owner * CHUNK + first + r * width + c + k
                    f_ref[pl.ds(at, count, stride=CHUNK), :] = dw[r * count : r * count + count, k * 128 : k * 128 + 128]

    place(0, m.n1[...], m.dqkv, pick, 3, 0)
    place(27, m.ctx[...], m.dh, pick, 3, 0)
    place(36, m.n2[...], m.de, pick, 3, 0)
    pick = picker(12)
    for b in range(4):
        place(72, m.act[:, b * D : b * D + D], m.gy, pick, 12, b * 32)
    lines = unsheared(table_pull(m.ds))
    zero = jnp.zeros((128, 128), f32)
    for j in range(108, CHUNK):
        f_ref[pl.ds(j, 128, stride=CHUNK), :] = zero
    for h in range(HEADS):
        for c in range(10):
            at = (h * 10 + c) * CHUNK + 108
            f_ref[at : at + 1, :] = lines[h][:, c * 128 : c * 128 + 128]
    mine = m.mine[0]

    def half(ref, offset):
        def step(i, carry):
            to = pl.ds(pl.multiple_of(i * CHUNK, CHUNK), CHUNK)
            ref[to, :] = f_ref[pl.ds(pl.multiple_of((2 * i + offset) * CHUNK, CHUNK), CHUNK), :].astype(bf16)
            return carry

        lax.fori_loop(0, 64, step, 0, unroll=8)

    half(m.give, 1 - mine)
    m.ready("give")
    half(m.keep, mine)
    m.ready("keep")


SQUARE = (HEADS, ROWS, ROWS)


def scr(shape, dtype):
    return pltpu.VMEM(shape, dtype)


def rows(width, space):
    return (ROWS, width), bf16, space


def run_first_forward(x, table, weights):
    return launch(
        first_forward,
        {"x": (x, "near"), "table": (table, "near")} | weights,
        {
            "n1": rows(D, "far"), "qkv": rows(3 * D, "far"), "p": (SQUARE, bf16, "far"), "ctx": rows(D, "far"),
            "h": rows(D, "far"), "n2": rows(D, "far"), "act": rows(FF, "far"), "slope": rows(FF, "far"),
            "y": rows(D, "near"),
        },
        {
            "bias": scr(SQUARE, f32), "turned": scr((D, ROWS), f32), "big": scr((ROWS, D), f32),
            "wide": scr((16, TPAD), f32),
        },
    )


def run_second(y, up, table, weights):
    return launch(
        second_whole,
        {"y": (y, "near"), "up": (up, "near"), "table": (table, "near")} | weights,
        {
            "n1": rows(D, "far"), "ctx": rows(D, "far"), "n2": rows(D, "far"), "act": rows(FF, "far"),
            "dqkv": rows(3 * D, "far"), "dh": rows(D, "far"), "de": rows(FF, "far"), "ds": (SQUARE, bf16, "far"),
            "gy": rows(D, "near"),
        },
        {
            "bias": scr(SQUARE, f32), "wide": scr((16, TPAD), f32),
            "qkv": scr((ROWS, 3 * D), bf16), "p": scr(SQUARE, bf16), "turned": scr((D, ROWS), f32),
            "h": scr((ROWS, D), bf16), "slope": scr((ROWS, FF), bf16), "dctx": scr((ROWS, D), bf16),
            "big": scr((ROWS, D), f32),
        },
    )


HALF = ((64 * CHUNK, 128), bf16, "far")


def run_first_backward(mine, gy, x, kept, weights):
    return launch(
        first_backward,
        {"mine": (mine, "flag"), "gy": (gy, "near"), "x": (x, "near"), "wc": weights["wc"]}
        | {"slope": (kept["slope"], "far"), "we": weights["we"], "h": (kept["h"], "far"), "wp": weights["wp"]}
        | {"qkv": (kept["qkv"], "far"), "p": (kept["p"], "far"), "wqkv": weights["wqkv"]}
        | {name: (kept[name], "far") for name in ("n1", "ctx", "n2", "act")},
        {"dx": rows(D, "near"), "keep": HALF, "give": HALF},
        {
            "turned": scr((D, ROWS), f32), "dctx": scr((ROWS, D), bf16), "big": scr((ROWS, D), f32),
            "dqkv": scr((ROWS, 3 * D), bf16), "dh": scr((ROWS, D), bf16), "de": scr((ROWS, FF), bf16),
            "ds": scr(SQUARE, bf16), "f": scr((128 * CHUNK, 128), f32),
        },
    )


def run_weights(mine, sums, gy, carried):
    return launch(
        weights_kernel,
        {"mine": (mine, "flag"), "gy": (gy, "near"), "carried": (carried, "near")}
        | {name: (sums[name], "far") for name in ("n1", "ctx", "n2", "act", "dqkv", "dh", "de", "ds")},
        {"keep": HALF, "give": HALF, "passed": (carried.shape, carried.dtype, "near")},
        {"f": scr((128 * CHUNK, 128), f32)},
    )


def passed_along(block, axis, distance):
    devices = range(lax.axis_size(axis))
    route = [((i - distance) % len(devices), i) for i in devices]
    return lax.ppermute(block, axis, route)


def edge_of(grid, dim, width, direction):
    extent = grid.shape[dim]
    if direction < 0:
        return lax.slice_in_dim(grid, 0, width, axis=dim)
    return lax.slice_in_dim(grid, extent - width, extent, axis=dim)


def rejoin(grid, dim, width, direction, arrived):
    extent = grid.shape[dim]
    if direction < 0:
        return jnp.concatenate([lax.slice_in_dim(grid, width, extent, axis=dim), arrived], axis=dim)
    return jnp.concatenate([arrived, lax.slice_in_dim(grid, 0, extent - width, axis=dim)], axis=dim)


def rolled_along(grid, dim, direction):
    width = (WT // 2, WH // 2, WW // 2)[dim]
    at = grid.ndim - 4 + dim
    moved = passed_along(edge_of(grid, at, width, direction), AXES[dim], direction)
    return rejoin(grid, at, width, direction, moved)


def to_rows(grid):
    return jnp.pad(grid, ((0, 0), (0, 0), (0, 1), (0, 0))).reshape(ROWS, D)


def to_grid(flat):
    return flat.reshape(WT, WH, PITCH, D)[:, :, :WW]


def swapped(block):
    return lax.ppermute(block, "wa", [(i, i ^ 1) for i in range(lax.axis_size("wa"))])


def scattered(kept, arrived):
    both = [
        (a.astype(f32) + b.astype(f32)).astype(bf16).reshape(64, CHUNK, 128) for a, b in zip(kept, arrived)
    ]
    groups = [[i for i in range(128) if i % 2 == side] for side in range(2)]
    spread = lax.all_to_all(
        jnp.concatenate(both, axis=1), AXES, 0, 0, axis_index_groups=groups, tiled=True
    )
    return jnp.sum(spread.astype(f32), axis=0)


def weight_parts(chunk):
    return (
        chunk[0:27].reshape(3, 3 * D),
        chunk[27:36].reshape(3, D),
        chunk[36:72].reshape(3, FF),
        chunk[72:108].reshape(12, D),
    )


def body(
    tokens, upstream, qkv_one, proj_one, table_one, expand_one, contract_one,
    qkv_two, proj_two, table_two, expand_two, contract_two,
):
    mine = (lax.axis_index("wa") % 2).astype(jnp.int32).reshape(1)
    x = to_rows(tokens)

    def far(wqkv, wp, we, wc):
        return {"wqkv": (wqkv, "far"), "wp": (wp, "far"), "we": (we, "far"), "wc": (wc, "far")}

    weights_one = far(qkv_one, proj_one, expand_one, contract_one)
    weights_two = far(qkv_two, proj_two, expand_two, contract_two)
    one = run_first_forward(x, table_one, weights_one)
    up = rolled_along(upstream, 0, -1)
    both = jnp.stack([rolled_along(to_grid(one["y"]), 0, -1), up])
    both = rolled_along(rolled_along(both, 1, -1), 2, -1)
    rolled, up = to_rows(both[0]), to_rows(both[1])
    two = run_second(rolled, up, table_two, weights_two)
    sent = passed_along(edge_of(to_grid(two["gy"]), 0, WT // 2, 1), "ta", 1)
    sums_two = run_weights(mine, two, up, two["gy"])
    gy = rejoin(to_grid(sums_two["passed"]), 0, WT // 2, 1, sent)
    gy = to_rows(rolled_along(rolled_along(gy, 1, 1), 2, 1))
    arrived_two = swapped(lax.dynamic_update_slice(sums_two["give"], gy[:1, :128], (CHUNK - 1, 0)))
    sums_one = run_first_backward(mine, gy, x, one, weights_one)
    keep_one, keep_two, give_one, dx = sums_one["keep"], sums_two["keep"], sums_one["give"], sums_one["dx"]
    total = scattered((keep_one, keep_two), (swapped(give_one), arrived_two))
    first, second = total[:CHUNK], total[CHUNK:]
    lines = jnp.concatenate([first[108:109], second[108:109]], axis=0)
    tables = lax.all_to_all(jnp.broadcast_to(lines[None], (128, 2, 128)), AXES, 0, 0, tiled=True)

    def table_of(which):
        return tables[:120, which].reshape(HEADS, TPAD)[:, :TABLE]

    g1, g2 = weight_parts(first), weight_parts(second)
    return (
        to_grid(dx), g1[0], g1[1], table_of(0), g1[2], g1[3],
        g2[0], g2[1], table_of(1), g2[2], g2[3],
    )


def solution(mesh):
    grid = P("ta", "ha", "wa", None)
    rows_split = P(AXES, None)
    return jax.shard_map(
        body,
        mesh=mesh,
        in_specs=(grid, grid) + (P(),) * 10,
        out_specs=(
            grid, rows_split, rows_split, P(), rows_split, rows_split,
            rows_split, rows_split, P(), rows_split, rows_split,
        ),
        check_vma=False,
    )
```

```python
import jax
import jax.numpy as jnp
from jax import lax
from jax.experimental import pallas as pl
from jax.experimental.pallas import tpu as pltpu
from jax.sharding import PartitionSpec as P

HEADS = 12
WT = 4
WH = 7
WW = 7
PITCH = 8
ROWS = WT * WH * PITCH
D = 384
FF = 1536
HD = 32
TABLE = 1183
TPAD = 1280
UPAD = 768
STEP = 32
CHUNK = 112
VMEM_LIMIT = 32 * 1024 * 1024
epsilon = 1e-05
f32 = jnp.float32
bf16 = jnp.bfloat16
NN = ((1,), (0,))
NT = ((1,), (1,))
AXES = ("ta", "ha", "wa")


def dot(a, b, dims):
    return lax.dot_general(a, b, (dims, ((), ())), preferred_element_type=f32)


class Held:
    def __init__(self, refs, incoming, outgoing):
        self.__dict__.update(refs)
        self.incoming = dict(incoming)
        self.outgoing = dict(outgoing)

    def need(self, *names):
        for name in names:
            if name in self.incoming:
                self.incoming.pop(name).wait()

    def ready(self, *names):
        for name in names:
            if name in self.outgoing:
                self.outgoing.pop(name).start()


def launch(kernel, ins, outs, scratch=()):
    places = {"parts": pltpu.HBM, "far": pltpu.HBM, "near": pltpu.VMEM, "flag": pltpu.SMEM, "pass": pltpu.HBM}
    passed = [n for n, (_, space) in ins.items() if space == "pass"]
    outs = dict(outs) | {n: (ins[n][0].shape, ins[n][0].dtype, "pass") for n in passed}
    scratch = dict(scratch)
    buffers = {}

    def copied(named, space, shape, dtype):
        cuts = {"far": 1, "parts": PIECES}.get(space, 0)
        size = shape[0] // max(cuts, 1)
        names = [named] if cuts == 1 else [f"{named}{i}" for i in range(cuts)]
        for name in names:
            buffers[name] = pltpu.VMEM((size,) + tuple(shape[1:]), dtype)
        return {name: (named, i * size, size) for i, name in enumerate(names)}

    far_ins, far_outs = {}, {}
    for n, (array, space) in ins.items():
        far_ins |= copied(n, space, array.shape, array.dtype)
    for n, (shape, dtype, space) in outs.items():
        far_outs |= copied(n, space, shape, dtype)

    def wrapped(*refs):
        named = dict(zip(list(ins) + list(outs), refs))
        rest = refs[len(ins) + len(outs) :]
        near = dict(zip(list(scratch) + list(buffers), rest))
        sems = rest[-1]
        incoming, outgoing = {}, {}
        for i, (n, (whole, first, size)) in enumerate(far_ins.items()):
            incoming[n] = pltpu.make_async_copy(named[whole].at[pl.ds(first, size)], near[n], sems.at[i])
            incoming[n].start()
        for i, (n, (whole, first, size)) in enumerate(far_outs.items()):
            cut = named[whole].at[pl.ds(first, size)]
            outgoing[n] = pltpu.make_async_copy(near[n], cut, sems.at[len(far_ins) + i])
        kernel(Held({**named, **near}, incoming, outgoing))
        for n in far_outs:
            outgoing[n].wait()

    results = pl.pallas_call(
        wrapped,
        out_shape=[
            pltpu.HBM(shape, dtype) if space in ("far", "parts", "pass") else jax.ShapeDtypeStruct(shape, dtype)
            for shape, dtype, space in outs.values()
        ],
        in_specs=[pl.BlockSpec(memory_space=places[space]) for _, space in ins.values()],
        out_specs=[pl.BlockSpec(memory_space=places[space]) for _, _, space in outs.values()],
        input_output_aliases={list(ins).index(n): list(outs).index(n) for n in passed},
        scratch_shapes=list(scratch.values())
        + list(buffers.values())
        + [pltpu.SemaphoreType.DMA((max(1, len(far_ins) + len(far_outs)),))],
        compiler_params=pltpu.CompilerParams(vmem_limit_bytes=VMEM_LIMIT),
    )(
        *[
            pltpu.with_memory_space_constraint(array, pltpu.HBM) if space in ("far", "parts", "pass") else array
            for array, space in ins.values()
        ]
    )
    return dict(zip(outs, results))


def row_steps():
    return range(0, ROWS, STEP)


def standardized(x):
    average = jnp.sum(x, axis=-1, keepdims=True) * (1.0 / D)
    centred = x - average
    spread = jnp.sum(centred * centred, axis=-1, keepdims=True) * (1.0 / D)
    scale = lax.rsqrt(spread + epsilon)
    return centred * scale, scale


def norm_pull(x, grad):
    unit, scale = standardized(x)
    mean_grad = jnp.sum(grad, axis=-1, keepdims=True) * (1.0 / D)
    mean_both = jnp.sum(grad * unit, axis=-1, keepdims=True) * (1.0 / D)
    return scale * (grad - mean_grad - unit * mean_both)


def norm_into(src, dst):
    for i in row_steps():
        rows = pl.ds(i, STEP)
        dst[rows, :] = standardized(src[rows, :].astype(f32))[0].astype(bf16)


def split3(x):
    hi = x.astype(bf16)
    rest = x - hi.astype(f32)
    mid = rest.astype(bf16)
    return hi, mid, (rest - mid.astype(f32)).astype(bf16)


def spread_onehot():
    col = lax.broadcasted_iota(jnp.int32, (1, UPAD), 1)
    group = lax.shift_right_logical(col, 3)
    w = jnp.bitwise_and(col, 7)
    valid = (w < WW) & (group < 91)
    target = jnp.where(valid, group * 13 + w + 6, -1)
    row = lax.broadcasted_iota(jnp.int32, (TPAD, UPAD), 0)
    return jnp.where(row == target, 1.0, 0.0).astype(bf16)


def build_bias(table_ref, bias_ref, wide_ref):
    wide_ref[...] = jnp.zeros_like(wide_ref)
    wide_ref[:HEADS, :TABLE] = table_ref[...]
    sheared = []
    for h in range(HEADS):
        line = jnp.broadcast_to(wide_ref[h : h + 1, :], (8, TPAD))
        sheared.append(pltpu.roll(line, 0, 1, stride=1, stride_axis=0))
    sheared = jnp.concatenate(sheared, axis=0)
    onehot = spread_onehot()
    hi, mid, lo = split3(sheared)
    u = dot(hi, onehot, NN) + dot(mid, onehot, NN) + dot(lo, onehot, NN)
    sub = lax.broadcasted_iota(jnp.int32, u.shape, 0)
    u = jnp.where(jnp.bitwise_and(sub, 7) == 7, -1e30, u)
    for hj in range(WH):
        base = (6 - hj) * 8
        y = jnp.concatenate([u[:, dt * 104 + base : dt * 104 + base + 56] for dt in range(7)], axis=1)
        for tj in range(WT):
            z = y[:, (3 - tj) * 56 : (3 - tj) * 56 + ROWS]
            bias_ref[:, tj * 56 + hj * 8 : tj * 56 + hj * 8 + 8, :] = z.reshape(HEADS, 8, ROWS)


def table_pull(ds_ref):
    du = jnp.zeros((HEADS * 8, UPAD), f32)
    for hj in range(WH):
        dy = jnp.zeros((HEADS * 8, 392), f32)
        for tj in range(WT):
            z = ds_ref[:, tj * 56 + hj * 8 : tj * 56 + hj * 8 + 8, :].astype(f32).reshape(HEADS * 8, ROWS)
            parts = []
            if tj < 3:
                parts.append(jnp.zeros((HEADS * 8, (3 - tj) * 56), f32))
            parts.append(z)
            if tj > 0:
                parts.append(jnp.zeros((HEADS * 8, tj * 56), f32))
            dy = dy + (jnp.concatenate(parts, axis=1) if len(parts) > 1 else parts[0])
        parts = []
        at = 0
        for dt in range(7):
            start = dt * 104 + (6 - hj) * 8
            if start > at:
                parts.append(jnp.zeros((HEADS * 8, start - at), f32))
            parts.append(dy[:, dt * 56 : dt * 56 + 56])
            at = start + 56
        parts.append(jnp.zeros((HEADS * 8, UPAD - at), f32))
        du = du + jnp.concatenate(parts, axis=1)
    onehot = spread_onehot()
    hi = du.astype(bf16)
    lo = (du - hi.astype(f32)).astype(bf16)
    return dot(hi, onehot, NT) + dot(lo, onehot, NT)


def unsheared(sheared):
    sub = jnp.bitwise_and(lax.broadcasted_iota(jnp.int32, sheared.shape, 0), 7)
    total = jnp.zeros_like(sheared)
    for wj in range(WW):
        moved = pltpu.roll(sheared, TPAD - wj, 1) if wj else sheared
        total = jnp.where(sub == wj, moved, total)
    return [jnp.sum(total[8 * h : 8 * h + 8], axis=0, keepdims=True) for h in range(HEADS)]


def head_mask(hh):
    lane = lax.broadcasted_iota(jnp.int32, (1, 128), 1)
    return (lane >= hh * HD) & (lane < hh * HD + HD)


def masked(value, hh):
    return jnp.where(head_mask(hh), value, jnp.zeros_like(value))


def attention_forward(n_ref, wqkv_ref, bias_ref, qkv_ref, p_ref, ctxt_ref, ctx_ref):
    for c in range(3):
        cols = slice(c * D, c * D + D)
        qkv_ref[:, cols] = dot(n_ref[...], wqkv_ref[:, cols], NN).astype(bf16)
    for g in range(3):
        lanes = slice(g * 128, g * 128 + 128)
        q = qkv_ref[:, g * 128 : g * 128 + 128]
        k = qkv_ref[:, D + g * 128 : D + g * 128 + 128]
        v = qkv_ref[:, 2 * D + g * 128 : 2 * D + g * 128 + 128]
        vt = v.astype(f32).T.astype(bf16)
        for hh in range(4):
            h = 4 * g + hh
            s = dot(k, masked(q, hh), NT) * (HD**-0.5) + bias_ref[h]
            top = jnp.max(s, axis=0, keepdims=True)
            e = jnp.exp(s - top)
            p = (e * (1.0 / jnp.sum(e, axis=0, keepdims=True))).astype(bf16)
            p_ref[h] = p
            ctxt_ref[h * HD : h * HD + HD, :] = dot(vt[hh * HD : hh * HD + HD], p, NN)
        ctx_ref[:, lanes] = ctxt_ref[g * 128 : g * 128 + 128, :].T.astype(bf16)


def attention_backward(dctx, qkv_ref, p_ref, ds_ref, dqt_ref, dqkv_ref):
    for g in range(3):
        q = qkv_ref[:, g * 128 : g * 128 + 128]
        k = qkv_ref[:, D + g * 128 : D + g * 128 + 128]
        v = qkv_ref[:, 2 * D + g * 128 : 2 * D + g * 128 + 128]
        dc = dctx[:, g * 128 : g * 128 + 128]
        kt = k.astype(f32).T.astype(bf16)
        dk = jnp.zeros((ROWS, 128), f32)
        dv = jnp.zeros((ROWS, 128), f32)
        for hh in range(4):
            h = 4 * g + hh
            dch = masked(dc, hh)
            p = p_ref[h]
            p32 = p.astype(f32)
            dp = dot(v, dch, NT)
            delta = jnp.sum(p32 * dp, axis=0, keepdims=True)
            ds = p32 * (dp - delta)
            ds_ref[h] = ds.astype(ds_ref.dtype)
            dsb = ds.astype(bf16)
            dv = dv + dot(p, dch, NN)
            dk = dk + dot(dsb, masked(q, hh), NN)
            dqt_ref[h * HD : h * HD + HD, :] = dot(kt[hh * HD : hh * HD + HD], dsb, NN)
        dq = dqt_ref[g * 128 : g * 128 + 128, :].T
        dqkv_ref[:, g * 128 : g * 128 + 128] = (dq * (HD**-0.5)).astype(bf16)
        dqkv_ref[:, D + g * 128 : D + g * 128 + 128] = (dk * (HD**-0.5)).astype(bf16)
        dqkv_ref[:, 2 * D + g * 128 : 2 * D + g * 128 + 128] = dv.astype(bf16)


def expand_gelu(n2_ref, we_ref, e_ref, act_ref, slope_ref):
    for c in range(4):
        cols = slice(c * D, c * D + D)
        e_ref[...] = dot(n2_ref[...], we_ref[:, cols], NN)
        for i in row_steps():
            rows = slice(i, i + STEP)
            x = e_ref[rows, :]
            cdf = 0.5 + 0.5 * lax.erf(x * 0.7071067811865476)
            act_ref[rows, cols] = (x * cdf).astype(bf16)
            slope = cdf + x * (jnp.exp(x * x * -0.5) * 0.3989422804014327)
            slope_ref[rows, cols] = slope.astype(slope_ref.dtype)


def attention_and_feed(m, x):
    m.need("wqkv")
    build_bias(m.table, m.bias, m.wide)
    norm_into(x, m.n1)
    attention_forward(m.n1, m.wqkv, m.bias, m.qkv, m.p, m.turned, m.ctx)
    m.need("wp", "we", "wc")
    m.ready("n1", "qkv", "p", "ctx")
    m.big[...] = dot(m.ctx[...], m.wp[...], NN)
    for i in row_steps():
        rows = slice(i, i + STEP)
        a = m.big[rows, :].astype(bf16).astype(f32)
        h = (x[rows, :].astype(f32) + a).astype(bf16)
        m.h[rows, :] = h
        m.n2[rows, :] = standardized(h.astype(f32))[0].astype(bf16)
    expand_gelu(m.n2, m.we, m.big, m.act, m.slope)
    m.ready("h", "n2", "act", "slope")


def first_forward(m):
    attention_and_feed(m, m.x)
    m.big[...] = dot(m.act[...], m.wc[...], NN)
    for i in row_steps():
        rows = slice(i, i + STEP)
        m.y[rows, :] = (m.h[rows, :].astype(f32) + m.big[rows, :]).astype(bf16)


def feed_backward(gy_ref, slope_ref, h_ref, we_ref, wc_ref, de_ref, big_ref, dh_ref):
    for c in range(4):
        cols = slice(c * D, c * D + D)
        big_ref[...] = dot(gy_ref[...], wc_ref[cols, :], NT)
        for i in row_steps():
            rows = slice(i, i + STEP)
            da = big_ref[rows, :].astype(bf16).astype(f32)
            de_ref[rows, cols] = (da * slope_ref[rows, cols].astype(f32)).astype(bf16)
    big_ref[...] = dot(de_ref[...], we_ref[...], NT)
    for i in row_steps():
        rows = slice(i, i + STEP)
        g = big_ref[rows, :].astype(bf16).astype(f32)
        back = norm_pull(h_ref[rows, :].astype(f32), g).astype(bf16)
        dh_ref[rows, :] = (gy_ref[rows, :].astype(f32) + back.astype(f32)).astype(bf16)


def attention_input_pull(x_ref, dqkv_ref, wqkv_ref, big_ref, dh_ref, dx_ref):
    big_ref[...] = dot(dqkv_ref[...], wqkv_ref[...], NT)
    for i in row_steps():
        rows = slice(i, i + STEP)
        g = big_ref[rows, :].astype(bf16).astype(f32)
        back = norm_pull(x_ref[rows, :].astype(f32), g).astype(bf16)
        dx_ref[rows, :] = (dh_ref[rows, :].astype(f32) + back.astype(f32)).astype(bf16)


def backward(m, x, gy, dx):
    m.need("wc", "slope", "we", "h")
    feed_backward(gy, m.slope, m.h, m.we, m.wc, m.de, m.big, m.dh)
    m.need("wp", "qkv", "p", "wqkv")
    m.dctx[...] = dot(m.dh[...], m.wp[...], NT).astype(bf16)
    attention_backward(m.dctx, m.qkv, m.p, m.ds, m.turned, m.dqkv)
    attention_input_pull(x, m.dqkv, m.wqkv, m.big, m.dh, dx)
    m.ready("ds", "dqkv", "de", "dh")


def second_whole(m):
    attention_and_feed(m, m.y)
    backward(m, m.y, m.up, m.gy)


def first_backward(m):
    backward(m, m.x, m.gy, m.dx)
    m.need("n1", "ctx", "n2", "act")
    weight_sums(m)


def picker(per):
    count = D // per
    row = lax.broadcasted_iota(jnp.int32, (D, 1), 0)
    r = jnp.zeros((D, 1), jnp.int32)
    for step in range(1, per):
        r = r + jnp.where(row >= step * count, 1, 0)
    target = (row - r * count) * per + r
    col = lax.broadcasted_iota(jnp.int32, (D, D), 1)
    return jnp.where(col == target, 1.0, 0.0).astype(bf16)


def weights_kernel(m):
    m.passed[...] = m.carried[...]
    m.need("n1", "dqkv", "ctx", "dh", "n2", "de", "act", "ds")
    weight_sums(m)


def weight_sums(m):
    f_ref = m.f
    pick = picker(3)

    def place(first, x, g_ref, pick, per, owner):
        width = g_ref.shape[1] // 128
        count = D // per
        xt = dot(pick, x, NT).astype(bf16)
        for c in range(0, width, 3):
            dw = dot(xt, g_ref[:, c * 128 : c * 128 + 384], NN)
            for r in range(per):
                for k in range(3):
                    at = owner * CHUNK + first + r * width + c + k
                    f_ref[pl.ds(at, count, stride=CHUNK), :] = dw[r * count : r * count + count, k * 128 : k * 128 + 128]

    place(0, m.n1[...], m.dqkv, pick, 3, 0)
    place(27, m.ctx[...], m.dh, pick, 3, 0)
    place(36, m.n2[...], m.de, pick, 3, 0)
    pick = picker(12)
    for b in range(4):
        place(72, m.act[:, b * D : b * D + D], m.gy, pick, 12, b * 32)
    lines = unsheared(table_pull(m.ds))
    zero = jnp.zeros((128, 128), f32)
    for j in range(108, CHUNK):
        f_ref[pl.ds(j, 128, stride=CHUNK), :] = zero
    for h in range(HEADS):
        for c in range(10):
            at = (h * 10 + c) * CHUNK + 108
            f_ref[at : at + 1, :] = lines[h][:, c * 128 : c * 128 + 128]
    mine = m.mine[0]

    def half(ref, offset):
        def step(i, carry):
            to = pl.ds(pl.multiple_of(i * CHUNK, CHUNK), CHUNK)
            ref[to, :] = f_ref[pl.ds(pl.multiple_of((2 * i + offset) * CHUNK, CHUNK), CHUNK), :].astype(bf16)
            return carry

        lax.fori_loop(0, 64, step, 0, unroll=8)

    half(m.give, 1 - mine)
    m.ready("give")
    half(m.keep, mine)
    m.ready("keep")


SQUARE = (HEADS, ROWS, ROWS)


def scr(shape, dtype):
    return pltpu.VMEM(shape, dtype)


def rows(width, space):
    return (ROWS, width), bf16, space


def run_first_forward(x, table, weights):
    return launch(
        first_forward,
        {"x": (x, "near"), "table": (table, "near")} | weights,
        {
            "n1": rows(D, "far"), "qkv": rows(3 * D, "far"), "p": (SQUARE, bf16, "far"), "ctx": rows(D, "far"),
            "h": rows(D, "far"), "n2": rows(D, "far"), "act": rows(FF, "far"), "slope": rows(FF, "far"),
            "y": rows(D, "near"),
        },
        {
            "bias": scr(SQUARE, f32), "turned": scr((D, ROWS), f32), "big": scr((ROWS, D), f32),
            "wide": scr((16, TPAD), f32),
        },
    )


def run_second(y, up, table, weights):
    return launch(
        second_whole,
        {"y": (y, "near"), "up": (up, "near"), "table": (table, "near")} | weights,
        {
            "n1": rows(D, "far"), "ctx": rows(D, "far"), "n2": rows(D, "far"), "act": rows(FF, "far"),
            "dqkv": rows(3 * D, "far"), "dh": rows(D, "far"), "de": rows(FF, "far"), "ds": (SQUARE, bf16, "far"),
            "gy": rows(D, "near"),
        },
        {
            "bias": scr(SQUARE, f32), "wide": scr((16, TPAD), f32),
            "qkv": scr((ROWS, 3 * D), bf16), "p": scr(SQUARE, bf16), "turned": scr((D, ROWS), f32),
            "h": scr((ROWS, D), bf16), "slope": scr((ROWS, FF), bf16), "dctx": scr((ROWS, D), bf16),
            "big": scr((ROWS, D), f32),
        },
    )


HALF = ((64 * CHUNK, 128), bf16, "far")


def run_first_backward(mine, gy, x, kept, weights, give_two):
    return launch(
        first_backward,
        {"mine": (mine, "flag"), "gy": (gy, "near"), "x": (x, "near"), "wc": weights["wc"]}
        | {"slope": (kept["slope"], "far"), "we": weights["we"], "h": (kept["h"], "far"), "wp": weights["wp"]}
        | {"qkv": (kept["qkv"], "far"), "p": (kept["p"], "far"), "wqkv": weights["wqkv"]}
        | {name: (kept[name], "far") for name in ("n1", "ctx", "n2", "act")}
        | {"give_two": (give_two, "pass")},
        {"dx": rows(D, "near"), "keep": HALF, "give": HALF},
        {
            "turned": scr((D, ROWS), f32), "dctx": scr((ROWS, D), bf16), "big": scr((ROWS, D), f32),
            "dqkv": scr((ROWS, 3 * D), bf16), "dh": scr((ROWS, D), bf16), "de": scr((ROWS, FF), bf16),
            "ds": scr(SQUARE, bf16), "f": scr((128 * CHUNK, 128), f32),
        },
    )


def run_weights(mine, sums, gy, carried):
    return launch(
        weights_kernel,
        {"mine": (mine, "flag"), "gy": (gy, "near"), "carried": (carried, "near")}
        | {name: (sums[name], "far") for name in ("n1", "ctx", "n2", "act", "dqkv", "dh", "de", "ds")},
        {"keep": HALF, "give": HALF, "passed": (carried.shape, carried.dtype, "near")},
        {"f": scr((128 * CHUNK, 128), f32)},
    )


PIECES = 4


def merge_kernel(m):
    per = 64 // PIECES
    for piece in range(PIECES):
        m.need(f"keep_one{piece}", f"keep_two{piece}")
        keeps = m.__dict__[f"keep_one{piece}"], m.__dict__[f"keep_two{piece}"]

        def step(j, carry):
            chunk = pl.ds(pl.multiple_of((piece * per + j) * CHUNK, CHUNK), CHUNK)
            own = pl.ds(pl.multiple_of(j * CHUNK, CHUNK), CHUNK)
            for b, (kept, arrived) in enumerate(zip(keeps, (m.arrived_one, m.arrived_two))):
                total = kept[own, :].astype(f32) + arrived[chunk, :].astype(f32)
                to = pl.ds(pl.multiple_of((2 * j + b) * CHUNK, CHUNK), CHUNK)
                m.__dict__[f"both{piece}"][to, :] = total.astype(bf16)
            return carry

        lax.fori_loop(0, per, step, 0, unroll=4)
        m.ready(f"both{piece}")


def run_merge(keep_one, keep_two, arrived_one, arrived_two):
    ins = {"keep_two": keep_two, "keep_one": keep_one}
    near = {"arrived_one": arrived_one, "arrived_two": arrived_two}
    both = launch(
        merge_kernel,
        {name: (array, "parts") for name, array in ins.items()} | {name: (array, "near") for name, array in near.items()},
        {"both": ((128 * CHUNK, 128), bf16, "parts")},
    )["both"]
    return both.reshape(64, 2 * CHUNK, 128)


def finish_kernel(m):
    per = 64 // PIECES
    total = None
    for piece in range(PIECES):
        m.need(f"spread{piece}")
        part = m.__dict__[f"spread{piece}"]

        def step(i, carry):
            return carry + part[i].astype(f32)

        total = lax.fori_loop(0, per, step, total if piece else jnp.zeros((2 * CHUNK, 128), f32), unroll=2)
    m.total[...] = total
    for b in range(2):
        at = b * CHUNK
        for name, first, count, width in (("qkv", 0, 3, 9), ("proj", 27, 3, 3), ("expand", 36, 3, 12), ("contract", 72, 12, 3)):
            target = m.__dict__[f"{name}_{b}"]
            for r in range(count):
                for c in range(width):
                    row = at + first + r * width + c
                    target[r : r + 1, c * 128 : c * 128 + 128] = m.total[row : row + 1, :]
        m.lines[:, b, :] = jnp.broadcast_to(m.total[at + 108 : at + 109, :], (128, 128))


def run_finish(spread):
    outs = {}
    for b in range(2):
        outs |= {f"qkv_{b}": ((3, 3 * D), f32, "near"), f"proj_{b}": ((3, D), f32, "near")}
        outs |= {f"expand_{b}": ((3, FF), f32, "near"), f"contract_{b}": ((12, D), f32, "near")}
    return launch(
        finish_kernel,
        {"spread": (spread, "parts")},
        outs | {"lines": ((128, 2, 128), f32, "near")},
        {"total": pltpu.VMEM((2 * CHUNK, 128), f32)},
    )


def passed_along(block, axis, distance):
    devices = range(lax.axis_size(axis))
    route = [((i - distance) % len(devices), i) for i in devices]
    return lax.ppermute(block, axis, route)


def edge_of(grid, dim, width, direction):
    extent = grid.shape[dim]
    if direction < 0:
        return lax.slice_in_dim(grid, 0, width, axis=dim)
    return lax.slice_in_dim(grid, extent - width, extent, axis=dim)


def rejoin(grid, dim, width, direction, arrived):
    extent = grid.shape[dim]
    if direction < 0:
        return jnp.concatenate([lax.slice_in_dim(grid, width, extent, axis=dim), arrived], axis=dim)
    return jnp.concatenate([arrived, lax.slice_in_dim(grid, 0, extent - width, axis=dim)], axis=dim)


def rolled_along(grid, dim, direction):
    width = (WT // 2, WH // 2, WW // 2)[dim]
    at = grid.ndim - 4 + dim
    moved = passed_along(edge_of(grid, at, width, direction), AXES[dim], direction)
    return rejoin(grid, at, width, direction, moved)


def to_rows(grid):
    return jnp.pad(grid, ((0, 0), (0, 0), (0, 1), (0, 0))).reshape(ROWS, D)


def to_grid(flat):
    return flat.reshape(WT, WH, PITCH, D)[:, :, :WW]


def swapped(block):
    return lax.ppermute(block, "wa", [(i, i ^ 1) for i in range(lax.axis_size("wa"))])


def exchanged(both):
    groups = [[i for i in range(128) if i % 2 == side] for side in range(2)]
    return lax.all_to_all(both, AXES, 0, 0, axis_index_groups=groups, tiled=True)


def body(
    tokens, upstream, qkv_one, proj_one, table_one, expand_one, contract_one,
    qkv_two, proj_two, table_two, expand_two, contract_two,
):
    mine = (lax.axis_index("wa") % 2).astype(jnp.int32).reshape(1)
    x = to_rows(tokens)

    def far(wqkv, wp, we, wc):
        return {"wqkv": (wqkv, "far"), "wp": (wp, "far"), "we": (we, "far"), "wc": (wc, "far")}

    weights_one = far(qkv_one, proj_one, expand_one, contract_one)
    weights_two = far(qkv_two, proj_two, expand_two, contract_two)
    one = run_first_forward(x, table_one, weights_one)
    both = jnp.stack([to_grid(one["y"]), upstream])
    for dim in range(3):
        both = rolled_along(both, dim, -1)
    rolled, up = to_rows(both[0]), to_rows(both[1])
    two = run_second(rolled, up, table_two, weights_two)
    gy = rolled_along(to_grid(two["gy"]), 0, 1)
    sent = passed_along(edge_of(gy, 1, WH // 2, 1), AXES[1], 1)
    sums_two = run_weights(mine, two, up, to_rows(gy))
    gy = rejoin(to_grid(sums_two["passed"]), 1, WH // 2, 1, sent)
    gy = to_rows(rolled_along(gy, 2, 1))
    sums_one = run_first_backward(mine, gy, x, one, weights_one, sums_two["give"])
    dx = sums_one["dx"]
    spread = exchanged(
        run_merge(sums_one["keep"], sums_two["keep"], swapped(sums_one["give"]), swapped(sums_one["give_two"]))
    )
    done = run_finish(spread)
    tables = lax.all_to_all(done["lines"], AXES, 0, 0, tiled=True)

    def table_of(which):
        return tables[:120, which].reshape(HEADS, TPAD)[:, :TABLE]

    g1, g2 = ([done[f"{name}_{b}"] for name in ("qkv", "proj", "expand", "contract")] for b in range(2))
    return (
        to_grid(dx), g1[0], g1[1], table_of(0), g1[2], g1[3],
        g2[0], g2[1], table_of(1), g2[2], g2[3],
    )


def solution(mesh):
    grid = P("ta", "ha", "wa", None)
    rows_split = P(AXES, None)
    return jax.shard_map(
        body,
        mesh=mesh,
        in_specs=(grid, grid) + (P(),) * 10,
        out_specs=(
            grid, rows_split, rows_split, P(), rows_split, rows_split,
            rows_split, rows_split, P(), rows_split, rows_split,
        ),
        check_vma=False,
    )
```

```python
import jax
import jax.numpy as jnp
from jax import lax
from jax.experimental import pallas as pl
from jax.experimental.pallas import tpu as pltpu
from jax.sharding import PartitionSpec as P

HEADS = 12
WT = 4
WH = 7
WW = 7
PITCH = 8
ROWS = WT * WH * PITCH
D = 384
FF = 1536
HD = 32
TABLE = 1183
TPAD = 1280
UPAD = 768
STEP = 32
CHUNK = 112
VMEM_LIMIT = 32 * 1024 * 1024
epsilon = 1e-05
f32 = jnp.float32
bf16 = jnp.bfloat16
NN = ((1,), (0,))
NT = ((1,), (1,))
AXES = ("ta", "ha", "wa")


def dot(a, b, dims):
    return lax.dot_general(a, b, (dims, ((), ())), preferred_element_type=f32)


class Held:
    def __init__(self, refs, incoming, outgoing):
        self.__dict__.update(refs)
        self.incoming = dict(incoming)
        self.outgoing = dict(outgoing)

    def need(self, *names):
        for name in names:
            if name in self.incoming:
                self.incoming.pop(name).wait()

    def ready(self, *names):
        for name in names:
            if name in self.outgoing:
                self.outgoing.pop(name).start()


def launch(kernel, ins, outs, scratch=()):
    places = {"parts": pltpu.HBM, "far": pltpu.HBM, "near": pltpu.VMEM, "flag": pltpu.SMEM, "pass": pltpu.HBM}
    passed = [n for n, (_, space) in ins.items() if space == "pass"]
    outs = dict(outs) | {n: (ins[n][0].shape, ins[n][0].dtype, "pass") for n in passed}
    scratch = dict(scratch)
    buffers = {}

    def copied(named, space, shape, dtype):
        cuts = {"far": 1, "parts": PIECES}.get(space, 0)
        size = shape[0] // max(cuts, 1)
        names = [named] if cuts == 1 else [f"{named}{i}" for i in range(cuts)]
        for name in names:
            buffers[name] = pltpu.VMEM((size,) + tuple(shape[1:]), dtype)
        return {name: (named, i * size, size) for i, name in enumerate(names)}

    far_ins, far_outs = {}, {}
    for n, (array, space) in ins.items():
        far_ins |= copied(n, space, array.shape, array.dtype)
    for n, (shape, dtype, space) in outs.items():
        far_outs |= copied(n, space, shape, dtype)

    def wrapped(*refs):
        named = dict(zip(list(ins) + list(outs), refs))
        rest = refs[len(ins) + len(outs) :]
        near = dict(zip(list(scratch) + list(buffers), rest))
        sems = rest[-1]
        incoming, outgoing = {}, {}
        for i, (n, (whole, first, size)) in enumerate(far_ins.items()):
            incoming[n] = pltpu.make_async_copy(named[whole].at[pl.ds(first, size)], near[n], sems.at[i])
            incoming[n].start()
        for i, (n, (whole, first, size)) in enumerate(far_outs.items()):
            cut = named[whole].at[pl.ds(first, size)]
            outgoing[n] = pltpu.make_async_copy(near[n], cut, sems.at[len(far_ins) + i])
        kernel(Held({**named, **near}, incoming, outgoing))
        for n in far_outs:
            outgoing[n].wait()

    results = pl.pallas_call(
        wrapped,
        out_shape=[
            pltpu.HBM(shape, dtype) if space in ("far", "parts", "pass") else jax.ShapeDtypeStruct(shape, dtype)
            for shape, dtype, space in outs.values()
        ],
        in_specs=[pl.BlockSpec(memory_space=places[space]) for _, space in ins.values()],
        out_specs=[pl.BlockSpec(memory_space=places[space]) for _, _, space in outs.values()],
        input_output_aliases={list(ins).index(n): list(outs).index(n) for n in passed},
        scratch_shapes=list(scratch.values())
        + list(buffers.values())
        + [pltpu.SemaphoreType.DMA((max(1, len(far_ins) + len(far_outs)),))],
        compiler_params=pltpu.CompilerParams(vmem_limit_bytes=VMEM_LIMIT),
    )(
        *[
            pltpu.with_memory_space_constraint(array, pltpu.HBM) if space in ("far", "parts", "pass") else array
            for array, space in ins.values()
        ]
    )
    return dict(zip(outs, results))


def row_steps():
    return range(0, ROWS, STEP)


def standardized(x):
    average = jnp.sum(x, axis=-1, keepdims=True) * (1.0 / D)
    centred = x - average
    spread = jnp.sum(centred * centred, axis=-1, keepdims=True) * (1.0 / D)
    scale = lax.rsqrt(spread + epsilon)
    return centred * scale, scale


def norm_pull(x, grad):
    unit, scale = standardized(x)
    mean_grad = jnp.sum(grad, axis=-1, keepdims=True) * (1.0 / D)
    mean_both = jnp.sum(grad * unit, axis=-1, keepdims=True) * (1.0 / D)
    return scale * (grad - mean_grad - unit * mean_both)


def norm_into(src, dst):
    for i in row_steps():
        rows = pl.ds(i, STEP)
        dst[rows, :] = standardized(src[rows, :].astype(f32))[0].astype(bf16)


def split3(x):
    hi = x.astype(bf16)
    rest = x - hi.astype(f32)
    mid = rest.astype(bf16)
    return hi, mid, (rest - mid.astype(f32)).astype(bf16)


def spread_onehot():
    col = lax.broadcasted_iota(jnp.int32, (1, UPAD), 1)
    group = lax.shift_right_logical(col, 3)
    w = jnp.bitwise_and(col, 7)
    valid = (w < WW) & (group < 91)
    target = jnp.where(valid, group * 13 + w + 6, -1)
    row = lax.broadcasted_iota(jnp.int32, (TPAD, UPAD), 0)
    return jnp.where(row == target, 1.0, 0.0).astype(bf16)


def build_bias(table_ref, bias_ref, wide_ref):
    wide_ref[...] = jnp.zeros_like(wide_ref)
    wide_ref[:HEADS, :TABLE] = table_ref[...]
    sheared = []
    for h in range(HEADS):
        line = jnp.broadcast_to(wide_ref[h : h + 1, :], (8, TPAD))
        sheared.append(pltpu.roll(line, 0, 1, stride=1, stride_axis=0))
    sheared = jnp.concatenate(sheared, axis=0)
    onehot = spread_onehot()
    hi, mid, lo = split3(sheared)
    u = dot(hi, onehot, NN) + dot(mid, onehot, NN) + dot(lo, onehot, NN)
    sub = lax.broadcasted_iota(jnp.int32, u.shape, 0)
    u = jnp.where(jnp.bitwise_and(sub, 7) == 7, -1e30, u)
    for hj in range(WH):
        base = (6 - hj) * 8
        y = jnp.concatenate([u[:, dt * 104 + base : dt * 104 + base + 56] for dt in range(7)], axis=1)
        for tj in range(WT):
            z = y[:, (3 - tj) * 56 : (3 - tj) * 56 + ROWS]
            bias_ref[:, tj * 56 + hj * 8 : tj * 56 + hj * 8 + 8, :] = z.reshape(HEADS, 8, ROWS)


def table_pull(ds_ref):
    du = jnp.zeros((HEADS * 8, UPAD), f32)
    for hj in range(WH):
        dy = jnp.zeros((HEADS * 8, 392), f32)
        for tj in range(WT):
            z = ds_ref[:, tj * 56 + hj * 8 : tj * 56 + hj * 8 + 8, :].reshape(HEADS * 8, ROWS)
            parts = []
            if tj < 3:
                parts.append(jnp.zeros((HEADS * 8, (3 - tj) * 56), f32))
            parts.append(z)
            if tj > 0:
                parts.append(jnp.zeros((HEADS * 8, tj * 56), f32))
            dy = dy + (jnp.concatenate(parts, axis=1) if len(parts) > 1 else parts[0])
        parts = []
        at = 0
        for dt in range(7):
            start = dt * 104 + (6 - hj) * 8
            if start > at:
                parts.append(jnp.zeros((HEADS * 8, start - at), f32))
            parts.append(dy[:, dt * 56 : dt * 56 + 56])
            at = start + 56
        parts.append(jnp.zeros((HEADS * 8, UPAD - at), f32))
        du = du + jnp.concatenate(parts, axis=1)
    onehot = spread_onehot()
    hi = du.astype(bf16)
    lo = (du - hi.astype(f32)).astype(bf16)
    return dot(hi, onehot, NT) + dot(lo, onehot, NT)


def unsheared(sheared):
    sub = jnp.bitwise_and(lax.broadcasted_iota(jnp.int32, sheared.shape, 0), 7)
    total = jnp.zeros_like(sheared)
    for wj in range(WW):
        moved = pltpu.roll(sheared, TPAD - wj, 1) if wj else sheared
        total = jnp.where(sub == wj, moved, total)
    return [jnp.sum(total[8 * h : 8 * h + 8], axis=0, keepdims=True) for h in range(HEADS)]


def head_mask(hh):
    lane = lax.broadcasted_iota(jnp.int32, (1, 128), 1)
    return (lane >= hh * HD) & (lane < hh * HD + HD)


def masked(value, hh):
    return jnp.where(head_mask(hh), value, jnp.zeros_like(value))


def attention_forward(n_ref, wqkv_ref, bias_ref, qkv_ref, p_ref, ctxt_ref, ctx_ref):
    for c in range(3):
        cols = slice(c * D, c * D + D)
        qkv_ref[:, cols] = dot(n_ref[...], wqkv_ref[:, cols], NN).astype(bf16)
    for g in range(3):
        lanes = slice(g * 128, g * 128 + 128)
        q = qkv_ref[:, g * 128 : g * 128 + 128]
        k = qkv_ref[:, D + g * 128 : D + g * 128 + 128]
        v = qkv_ref[:, 2 * D + g * 128 : 2 * D + g * 128 + 128]
        vt = v.astype(f32).T.astype(bf16)
        for hh in range(4):
            h = 4 * g + hh
            s = dot(k, masked(q, hh), NT) * (HD**-0.5) + bias_ref[h]
            top = jnp.max(s, axis=0, keepdims=True)
            e = jnp.exp(s - top)
            p = (e * (1.0 / jnp.sum(e, axis=0, keepdims=True))).astype(bf16)
            p_ref[h] = p
            ctxt_ref[h * HD : h * HD + HD, :] = dot(vt[hh * HD : hh * HD + HD], p, NN)
        ctx_ref[:, lanes] = ctxt_ref[g * 128 : g * 128 + 128, :].T.astype(bf16)


def attention_backward(dctx, qkv_ref, p_ref, ds_ref, dqt_ref, dqkv_ref):
    for g in range(3):
        q = qkv_ref[:, g * 128 : g * 128 + 128]
        k = qkv_ref[:, D + g * 128 : D + g * 128 + 128]
        v = qkv_ref[:, 2 * D + g * 128 : 2 * D + g * 128 + 128]
        dc = dctx[:, g * 128 : g * 128 + 128]
        kt = k.astype(f32).T.astype(bf16)
        dk = jnp.zeros((ROWS, 128), f32)
        dv = jnp.zeros((ROWS, 128), f32)
        for hh in range(4):
            h = 4 * g + hh
            dch = masked(dc, hh)
            p = p_ref[h]
            p32 = p.astype(f32)
            dp = dot(v, dch, NT)
            delta = jnp.sum(p32 * dp, axis=0, keepdims=True)
            ds = p32 * (dp - delta)
            ds_ref[h] = ds.astype(ds_ref.dtype)
            dsb = ds.astype(bf16)
            dv = dv + dot(p, dch, NN)
            dk = dk + dot(dsb, masked(q, hh), NN)
            dqt_ref[h * HD : h * HD + HD, :] = dot(kt[hh * HD : hh * HD + HD], dsb, NN)
        dq = dqt_ref[g * 128 : g * 128 + 128, :].T
        dqkv_ref[:, g * 128 : g * 128 + 128] = (dq * (HD**-0.5)).astype(bf16)
        dqkv_ref[:, D + g * 128 : D + g * 128 + 128] = (dk * (HD**-0.5)).astype(bf16)
        dqkv_ref[:, 2 * D + g * 128 : 2 * D + g * 128 + 128] = dv.astype(bf16)


def expand_gelu(n2_ref, we_ref, e_ref, act_ref, slope_ref):
    for c in range(4):
        cols = slice(c * D, c * D + D)
        e_ref[...] = dot(n2_ref[...], we_ref[:, cols], NN)
        for i in row_steps():
            rows = slice(i, i + STEP)
            x = e_ref[rows, :]
            cdf = 0.5 + 0.5 * lax.erf(x * 0.7071067811865476)
            act_ref[rows, cols] = (x * cdf).astype(bf16)
            slope = cdf + x * (jnp.exp(x * x * -0.5) * 0.3989422804014327)
            slope_ref[rows, cols] = slope.astype(slope_ref.dtype)


def attention_and_feed(m, x):
    m.need("table", "wqkv")
    build_bias(m.table, m.bias, m.wide)
    norm_into(x, m.n1)
    attention_forward(m.n1, m.wqkv, m.bias, m.qkv, m.p, m.turned, m.ctx)
    m.need("wp", "we", "wc")
    m.ready("n1", "qkv", "p", "ctx")
    m.big[...] = dot(m.ctx[...], m.wp[...], NN)
    for i in row_steps():
        rows = slice(i, i + STEP)
        a = m.big[rows, :].astype(bf16).astype(f32)
        h = (x[rows, :].astype(f32) + a).astype(bf16)
        m.h[rows, :] = h
        m.n2[rows, :] = standardized(h.astype(f32))[0].astype(bf16)
    expand_gelu(m.n2, m.we, m.big, m.act, m.slope)
    m.ready("h", "n2", "act", "slope")


def first_forward(m):
    attention_and_feed(m, m.x)
    m.big[...] = dot(m.act[...], m.wc[...], NN)
    for i in row_steps():
        rows = slice(i, i + STEP)
        m.y[rows, :] = (m.h[rows, :].astype(f32) + m.big[rows, :]).astype(bf16)


def feed_backward(gy_ref, slope_ref, h_ref, we_ref, wc_ref, de_ref, big_ref, dh_ref):
    for c in range(4):
        cols = slice(c * D, c * D + D)
        big_ref[...] = dot(gy_ref[...], wc_ref[cols, :], NT)
        for i in row_steps():
            rows = slice(i, i + STEP)
            da = big_ref[rows, :].astype(bf16).astype(f32)
            de_ref[rows, cols] = (da * slope_ref[rows, cols].astype(f32)).astype(bf16)
    big_ref[...] = dot(de_ref[...], we_ref[...], NT)
    for i in row_steps():
        rows = slice(i, i + STEP)
        g = big_ref[rows, :].astype(bf16).astype(f32)
        back = norm_pull(h_ref[rows, :].astype(f32), g).astype(bf16)
        dh_ref[rows, :] = (gy_ref[rows, :].astype(f32) + back.astype(f32)).astype(bf16)


def attention_input_pull(x_ref, dqkv_ref, wqkv_ref, big_ref, dh_ref, dx_ref):
    big_ref[...] = dot(dqkv_ref[...], wqkv_ref[...], NT)
    for i in row_steps():
        rows = slice(i, i + STEP)
        g = big_ref[rows, :].astype(bf16).astype(f32)
        back = norm_pull(x_ref[rows, :].astype(f32), g).astype(bf16)
        dx_ref[rows, :] = (dh_ref[rows, :].astype(f32) + back.astype(f32)).astype(bf16)


def backward(m, x, gy, dx):
    m.need("wc", "slope", "we", "h")
    feed_backward(gy, m.slope, m.h, m.we, m.wc, m.de, m.big, m.dh)
    m.need("wp", "qkv", "p", "wqkv")
    m.dctx[...] = dot(m.dh[...], m.wp[...], NT).astype(bf16)
    attention_backward(m.dctx, m.qkv, m.p, m.ds, m.turned, m.dqkv)
    attention_input_pull(x, m.dqkv, m.wqkv, m.big, m.dh, dx)
    m.ready("ds", "dqkv", "de", "dh")


def second_whole(m):
    attention_and_feed(m, m.y)
    backward(m, m.y, m.up, m.gy)


def first_backward(m):
    backward(m, m.x, m.gy, m.dx)
    m.need("n1", "ctx", "n2", "act")
    weight_sums(m, m.ds)


def picker(per):
    count = D // per
    row = lax.broadcasted_iota(jnp.int32, (D, 1), 0)
    r = jnp.zeros((D, 1), jnp.int32)
    for step in range(1, per):
        r = r + jnp.where(row >= step * count, 1, 0)
    target = (row - r * count) * per + r
    col = lax.broadcasted_iota(jnp.int32, (D, D), 1)
    return jnp.where(col == target, 1.0, 0.0).astype(bf16)


def weights_kernel(m):
    m.passed[...] = m.carried[...]
    m.need("n1", "dqkv", "ctx", "dh", "n2", "de", "act", "ds")
    for h in range(HEADS):
        m.wide[h] = m.ds[h].astype(f32)
    weight_sums(m, m.wide)


def weight_sums(m, ds):
    f_ref = m.f
    pick = picker(3)

    def place(first, x, g_ref, pick, per, owner):
        width = g_ref.shape[1] // 128
        count = D // per
        xt = dot(pick, x, NT).astype(bf16)
        for c in range(0, width, 3):
            dw = dot(xt, g_ref[:, c * 128 : c * 128 + 384], NN)
            for r in range(per):
                for k in range(3):
                    at = owner * CHUNK + first + r * width + c + k
                    f_ref[pl.ds(at, count, stride=CHUNK), :] = dw[r * count : r * count + count, k * 128 : k * 128 + 128]

    place(0, m.n1[...], m.dqkv, pick, 3, 0)
    place(27, m.ctx[...], m.dh, pick, 3, 0)
    place(36, m.n2[...], m.de, pick, 3, 0)
    pick = picker(12)
    for b in range(4):
        place(72, m.act[:, b * D : b * D + D], m.gy, pick, 12, b * 32)
    lines = unsheared(table_pull(ds))
    zero = jnp.zeros((128, 128), f32)
    for j in range(108, CHUNK):
        f_ref[pl.ds(j, 128, stride=CHUNK), :] = zero
    for h in range(HEADS):
        for c in range(10):
            at = (h * 10 + c) * CHUNK + 108
            f_ref[at : at + 1, :] = lines[h][:, c * 128 : c * 128 + 128]
    mine = m.mine[0]

    def half(ref, offset):
        def step(i, carry):
            to = pl.ds(pl.multiple_of(i * CHUNK, CHUNK), CHUNK)
            ref[to, :] = f_ref[pl.ds(pl.multiple_of((2 * i + offset) * CHUNK, CHUNK), CHUNK), :].astype(bf16)
            return carry

        lax.fori_loop(0, 64, step, 0, unroll=8)

    half(m.give, 1 - mine)
    m.ready("give")
    half(m.keep, mine)
    m.ready("keep")


SQUARE = (HEADS, ROWS, ROWS)


def scr(shape, dtype):
    return pltpu.VMEM(shape, dtype)


def rows(width, space):
    return (ROWS, width), bf16, space


def run_first_forward(x, table, weights):
    return launch(
        first_forward,
        {"x": (x, "near"), "table": (table, "far")} | weights,
        {
            "n1": rows(D, "far"), "qkv": rows(3 * D, "far"), "p": (SQUARE, bf16, "far"), "ctx": rows(D, "far"),
            "h": rows(D, "far"), "n2": rows(D, "far"), "act": rows(FF, "far"), "slope": rows(FF, "far"),
            "y": rows(D, "near"),
        },
        {
            "bias": scr(SQUARE, f32), "turned": scr((D, ROWS), f32), "big": scr((ROWS, D), f32),
            "wide": scr((16, TPAD), f32),
        },
    )


def run_second(y, up, table, weights):
    return launch(
        second_whole,
        {"y": (y, "near"), "up": (up, "near"), "table": (table, "near")} | weights,
        {
            "n1": rows(D, "far"), "ctx": rows(D, "far"), "n2": rows(D, "far"), "act": rows(FF, "far"),
            "dqkv": rows(3 * D, "far"), "dh": rows(D, "far"), "de": rows(FF, "far"), "ds": (SQUARE, bf16, "far"),
            "gy": rows(D, "near"),
        },
        {
            "bias": scr(SQUARE, f32), "wide": scr((16, TPAD), f32),
            "qkv": scr((ROWS, 3 * D), bf16), "p": scr(SQUARE, bf16), "turned": scr((D, ROWS), f32),
            "h": scr((ROWS, D), bf16), "slope": scr((ROWS, FF), bf16), "dctx": scr((ROWS, D), bf16),
            "big": scr((ROWS, D), f32),
        },
    )


HALF = ((64 * CHUNK, 128), bf16, "far")


def run_first_backward(mine, gy, x, kept, weights, give_two):
    return launch(
        first_backward,
        {"mine": (mine, "flag"), "gy": (gy, "near"), "x": (x, "near"), "wc": (weights["wc"][0], "near")}
        | {"slope": (kept["slope"], "near"), "we": (weights["we"][0], "near"), "h": (kept["h"], "near")}
        | {"wp": weights["wp"]}
        | {"qkv": (kept["qkv"], "far"), "p": (kept["p"], "far"), "wqkv": weights["wqkv"]}
        | {name: (kept[name], "far") for name in ("n1", "ctx", "n2", "act")}
        | {"give_two": (give_two, "pass")},
        {"dx": rows(D, "near"), "keep": HALF, "give": HALF},
        {
            "turned": scr((D, ROWS), f32), "dctx": scr((ROWS, D), bf16), "big": scr((ROWS, D), f32),
            "dqkv": scr((ROWS, 3 * D), bf16), "dh": scr((ROWS, D), bf16), "de": scr((ROWS, FF), bf16),
            "ds": scr(SQUARE, f32), "f": scr((128 * CHUNK, 128), f32),
        },
    )


def run_weights(mine, sums, gy, carried):
    return launch(
        weights_kernel,
        {"mine": (mine, "flag"), "gy": (gy, "near"), "carried": (carried, "near")}
        | {name: (sums[name], "far") for name in ("n1", "ctx", "n2", "act", "dqkv", "dh", "de", "ds")},
        {"keep": HALF, "give": HALF, "passed": (carried.shape, carried.dtype, "near")},
        {"f": scr((128 * CHUNK, 128), f32), "wide": scr(SQUARE, f32)},
    )


PIECES = 4


def merge_kernel(m):
    per = 64 // PIECES
    for piece in range(PIECES):
        m.need(f"keep_one{piece}", f"keep_two{piece}")
        keeps = m.__dict__[f"keep_one{piece}"], m.__dict__[f"keep_two{piece}"]

        def step(j, carry):
            chunk = pl.ds(pl.multiple_of((piece * per + j) * CHUNK, CHUNK), CHUNK)
            own = pl.ds(pl.multiple_of(j * CHUNK, CHUNK), CHUNK)
            for b, (kept, arrived) in enumerate(zip(keeps, (m.arrived_one, m.arrived_two))):
                total = kept[own, :].astype(f32) + arrived[chunk, :].astype(f32)
                to = pl.ds(pl.multiple_of((2 * j + b) * CHUNK, CHUNK), CHUNK)
                m.__dict__[f"both{piece}"][to, :] = total.astype(bf16)
            return carry

        lax.fori_loop(0, per, step, 0, unroll=4)
        m.ready(f"both{piece}")


def run_merge(keep_one, keep_two, arrived_one, arrived_two):
    ins = {"keep_two": keep_two, "keep_one": keep_one}
    near = {"arrived_one": arrived_one, "arrived_two": arrived_two}
    both = launch(
        merge_kernel,
        {name: (array, "parts") for name, array in ins.items()} | {name: (array, "near") for name, array in near.items()},
        {"both": ((128 * CHUNK, 128), bf16, "parts")},
    )["both"]
    return both.reshape(64, 2 * CHUNK, 128)


def finish_kernel(m):
    per = 64 // PIECES
    total = None
    for piece in range(PIECES):
        m.need(f"spread{piece}")
        part = m.__dict__[f"spread{piece}"]

        def step(i, carry):
            return carry + part[i].astype(f32)

        total = lax.fori_loop(0, per, step, total if piece else jnp.zeros((2 * CHUNK, 128), f32), unroll=2)
    m.total[...] = total
    for b in range(2):
        at = b * CHUNK
        for name, first, count, width in (("qkv", 0, 3, 9), ("proj", 27, 3, 3), ("expand", 36, 3, 12), ("contract", 72, 12, 3)):
            target = m.__dict__[f"{name}_{b}"]
            for r in range(count):
                for c in range(width):
                    row = at + first + r * width + c
                    target[r : r + 1, c * 128 : c * 128 + 128] = m.total[row : row + 1, :]
        m.lines[:, b, :] = jnp.broadcast_to(m.total[at + 108 : at + 109, :], (128, 128))


def run_finish(spread):
    outs = {}
    for b in range(2):
        outs |= {f"qkv_{b}": ((3, 3 * D), f32, "near"), f"proj_{b}": ((3, D), f32, "near")}
        outs |= {f"expand_{b}": ((3, FF), f32, "near"), f"contract_{b}": ((12, D), f32, "near")}
    return launch(
        finish_kernel,
        {"spread": (spread, "parts")},
        outs | {"lines": ((128, 2, 128), f32, "near")},
        {"total": pltpu.VMEM((2 * CHUNK, 128), f32)},
    )


def passed_along(block, axis, distance):
    devices = range(lax.axis_size(axis))
    route = [((i - distance) % len(devices), i) for i in devices]
    return lax.ppermute(block, axis, route)


def edge_of(grid, dim, width, direction):
    extent = grid.shape[dim]
    if direction < 0:
        return lax.slice_in_dim(grid, 0, width, axis=dim)
    return lax.slice_in_dim(grid, extent - width, extent, axis=dim)


def rejoin(grid, dim, width, direction, arrived):
    extent = grid.shape[dim]
    if direction < 0:
        return jnp.concatenate([lax.slice_in_dim(grid, width, extent, axis=dim), arrived], axis=dim)
    return jnp.concatenate([arrived, lax.slice_in_dim(grid, 0, extent - width, axis=dim)], axis=dim)


def rolled_along(grid, dim, direction):
    width = (WT // 2, WH // 2, WW // 2)[dim]
    at = grid.ndim - 4 + dim
    moved = passed_along(edge_of(grid, at, width, direction), AXES[dim], direction)
    return rejoin(grid, at, width, direction, moved)


def rolled_twice(grid, direction):
    first = grid.ndim - 4
    sizes = [lax.axis_size(axis) for axis in AXES[:2]]
    parts = {}
    for bt in range(2):
        for bh in range(2):
            part = grid
            for at, width, moves in ((first, WT // 2, bt), (first + 1, WH // 2, bh)):
                extent = part.shape[at]
                if moves:
                    part = edge_of(part, at, width, direction)
                elif direction < 0:
                    part = lax.slice_in_dim(part, width, extent, axis=at)
                else:
                    part = lax.slice_in_dim(part, 0, extent - width, axis=at)
            if bt or bh:
                route = [
                    (t * sizes[1] + h, (t + bt * direction) % sizes[0] * sizes[1] + (h + bh * direction) % sizes[1])
                    for t in range(sizes[0])
                    for h in range(sizes[1])
                ]
                part = lax.ppermute(part, AXES[:2], route)
            parts[bt, bh] = part
    order = (0, 1) if direction < 0 else (1, 0)
    halves = [jnp.concatenate([parts[bt, bh] for bh in order], axis=first + 1) for bt in order]
    return jnp.concatenate(halves, axis=first)


def to_rows(grid):
    return jnp.pad(grid, ((0, 0), (0, 0), (0, 1), (0, 0))).reshape(ROWS, D)


def to_grid(flat):
    return flat.reshape(WT, WH, PITCH, D)[:, :, :WW]


def swapped(block):
    return lax.ppermute(block, "wa", [(i, i ^ 1) for i in range(lax.axis_size("wa"))])


def exchanged(both):
    groups = [[i for i in range(128) if i % 2 == side] for side in range(2)]
    return lax.all_to_all(both, AXES, 0, 0, axis_index_groups=groups, tiled=True)


def body(
    tokens, upstream, qkv_one, proj_one, table_one, expand_one, contract_one,
    qkv_two, proj_two, table_two, expand_two, contract_two,
):
    mine = (lax.axis_index("wa") % 2).astype(jnp.int32).reshape(1)
    x = to_rows(tokens)

    def far(wqkv, wp, we, wc):
        return {"wqkv": (wqkv, "far"), "wp": (wp, "far"), "we": (we, "far"), "wc": (wc, "far")}

    weights_one = far(qkv_one, proj_one, expand_one, contract_one)
    weights_two = far(qkv_two, proj_two, expand_two, contract_two)
    one = run_first_forward(x, table_one, weights_one)
    both = jnp.stack([to_grid(one["y"]), upstream])
    both = rolled_along(rolled_twice(both, -1), 2, -1)
    rolled, up = to_rows(both[0]), to_rows(both[1])
    two = run_second(rolled, up, table_two, {name: (w, "near") for name, (w, _) in weights_two.items()})
    gy = rolled_twice(to_grid(two["gy"]), 1)
    sent = passed_along(edge_of(gy, 2, WW // 2, 1), AXES[2], 1)
    sums_two = run_weights(mine, two, up, to_rows(gy))
    gy = to_rows(rejoin(to_grid(sums_two["passed"]), 2, WW // 2, 1, sent))
    sums_one = run_first_backward(mine, gy, x, one, weights_one, sums_two["give"])
    dx = sums_one["dx"]
    spread = exchanged(
        run_merge(sums_one["keep"], sums_two["keep"], swapped(sums_one["give"]), swapped(sums_one["give_two"]))
    )
    done = run_finish(spread)
    tables = lax.all_to_all(done["lines"], AXES, 0, 0, tiled=True)

    def table_of(which):
        return tables[:120, which].reshape(HEADS, TPAD)[:, :TABLE]

    g1, g2 = ([done[f"{name}_{b}"] for name in ("qkv", "proj", "expand", "contract")] for b in range(2))
    return (
        to_grid(dx), g1[0], g1[1], table_of(0), g1[2], g1[3],
        g2[0], g2[1], table_of(1), g2[2], g2[3],
    )


def solution(mesh):
    grid = P("ta", "ha", "wa", None)
    rows_split = P(AXES, None)
    return jax.shard_map(
        body,
        mesh=mesh,
        in_specs=(grid, grid) + (P(),) * 10,
        out_specs=(
            grid, rows_split, rows_split, P(), rows_split, rows_split,
            rows_split, rows_split, P(), rows_split, rows_split,
        ),
        check_vma=False,
    )
```

```python
import jax
import jax.numpy as jnp
from jax import lax
from jax.experimental import pallas as pl
from jax.experimental.pallas import tpu as pltpu
from jax.sharding import PartitionSpec as P

HEADS = 12
WT = 4
WH = 7
WW = 7
PITCH = 8
ROWS = WT * WH * PITCH
D = 384
FF = 1536
HD = 32
TABLE = 1183
TPAD = 1280
UPAD = 768
STEP = 32
CHUNK = 112
VMEM_LIMIT = 32 * 1024 * 1024
epsilon = 1e-05
f32 = jnp.float32
bf16 = jnp.bfloat16
NN = ((1,), (0,))
NT = ((1,), (1,))
AXES = ("ta", "ha", "wa")


def dot(a, b, dims):
    return lax.dot_general(a, b, (dims, ((), ())), preferred_element_type=f32)


class Held:
    def __init__(self, refs, incoming, outgoing):
        self.__dict__.update(refs)
        self.incoming = dict(incoming)
        self.outgoing = dict(outgoing)

    def need(self, *names):
        for name in names:
            if name in self.incoming:
                self.incoming.pop(name).wait()

    def ready(self, *names):
        for name in names:
            if name in self.outgoing:
                self.outgoing.pop(name).start()


def launch(kernel, ins, outs, scratch=()):
    places = {"parts": pltpu.HBM, "far": pltpu.HBM, "near": pltpu.VMEM, "flag": pltpu.SMEM, "pass": pltpu.HBM}
    passed = [n for n, (_, space) in ins.items() if space == "pass"]
    outs = dict(outs) | {n: (ins[n][0].shape, ins[n][0].dtype, "pass") for n in passed}
    scratch = dict(scratch)
    buffers = {}

    def copied(named, space, shape, dtype):
        cuts = {"far": 1, "parts": PIECES}.get(space, 0)
        size = shape[0] // max(cuts, 1)
        names = [named] if cuts == 1 else [f"{named}{i}" for i in range(cuts)]
        for name in names:
            buffers[name] = pltpu.VMEM((size,) + tuple(shape[1:]), dtype)
        return {name: (named, i * size, size) for i, name in enumerate(names)}

    far_ins, far_outs = {}, {}
    for n, (array, space) in ins.items():
        far_ins |= copied(n, space, array.shape, array.dtype)
    for n, (shape, dtype, space) in outs.items():
        far_outs |= copied(n, space, shape, dtype)

    def wrapped(*refs):
        named = dict(zip(list(ins) + list(outs), refs))
        rest = refs[len(ins) + len(outs) :]
        near = dict(zip(list(scratch) + list(buffers), rest))
        sems = rest[-1]
        incoming, outgoing = {}, {}
        for i, (n, (whole, first, size)) in enumerate(far_ins.items()):
            incoming[n] = pltpu.make_async_copy(named[whole].at[pl.ds(first, size)], near[n], sems.at[i])
            incoming[n].start()
        for i, (n, (whole, first, size)) in enumerate(far_outs.items()):
            cut = named[whole].at[pl.ds(first, size)]
            outgoing[n] = pltpu.make_async_copy(near[n], cut, sems.at[len(far_ins) + i])
        kernel(Held({**named, **near}, incoming, outgoing))
        for n in far_outs:
            outgoing[n].wait()

    results = pl.pallas_call(
        wrapped,
        out_shape=[
            pltpu.HBM(shape, dtype) if space in ("far", "parts", "pass") else jax.ShapeDtypeStruct(shape, dtype)
            for shape, dtype, space in outs.values()
        ],
        in_specs=[pl.BlockSpec(memory_space=places[space]) for _, space in ins.values()],
        out_specs=[pl.BlockSpec(memory_space=places[space]) for _, _, space in outs.values()],
        input_output_aliases={list(ins).index(n): list(outs).index(n) for n in passed},
        scratch_shapes=list(scratch.values())
        + list(buffers.values())
        + [pltpu.SemaphoreType.DMA((max(1, len(far_ins) + len(far_outs)),))],
        compiler_params=pltpu.CompilerParams(vmem_limit_bytes=VMEM_LIMIT),
    )(
        *[
            pltpu.with_memory_space_constraint(array, pltpu.HBM) if space in ("far", "parts", "pass") else array
            for array, space in ins.values()
        ]
    )
    return dict(zip(outs, results))


def row_steps():
    return range(0, ROWS, STEP)


def standardized(x):
    average = jnp.sum(x, axis=-1, keepdims=True) * (1.0 / D)
    centred = x - average
    spread = jnp.sum(centred * centred, axis=-1, keepdims=True) * (1.0 / D)
    scale = lax.rsqrt(spread + epsilon)
    return centred * scale, scale


def norm_pull(x, grad):
    unit, scale = standardized(x)
    mean_grad = jnp.sum(grad, axis=-1, keepdims=True) * (1.0 / D)
    mean_both = jnp.sum(grad * unit, axis=-1, keepdims=True) * (1.0 / D)
    return scale * (grad - mean_grad - unit * mean_both)


def norm_into(src, dst):
    for i in row_steps():
        rows = pl.ds(i, STEP)
        dst[rows, :] = standardized(src[rows, :].astype(f32))[0].astype(bf16)


def split3(x):
    hi = x.astype(bf16)
    rest = x - hi.astype(f32)
    mid = rest.astype(bf16)
    return hi, mid, (rest - mid.astype(f32)).astype(bf16)


def spread_onehot():
    col = lax.broadcasted_iota(jnp.int32, (1, UPAD), 1)
    group = lax.shift_right_logical(col, 3)
    w = jnp.bitwise_and(col, 7)
    valid = (w < WW) & (group < 91)
    target = jnp.where(valid, group * 13 + w + 6, -1)
    row = lax.broadcasted_iota(jnp.int32, (TPAD, UPAD), 0)
    return jnp.where(row == target, 1.0, 0.0).astype(bf16)


def build_bias(table_ref, bias_ref, wide_ref):
    wide_ref[...] = jnp.zeros_like(wide_ref)
    wide_ref[:HEADS, :TABLE] = table_ref[...]
    sheared = []
    for h in range(HEADS):
        line = jnp.broadcast_to(wide_ref[h : h + 1, :], (8, TPAD))
        sheared.append(pltpu.roll(line, 0, 1, stride=1, stride_axis=0))
    sheared = jnp.concatenate(sheared, axis=0)
    onehot = spread_onehot()
    hi, mid, lo = split3(sheared)
    u = dot(hi, onehot, NN) + dot(mid, onehot, NN) + dot(lo, onehot, NN)
    sub = lax.broadcasted_iota(jnp.int32, u.shape, 0)
    u = jnp.where(jnp.bitwise_and(sub, 7) == 7, -1e30, u)
    for hj in range(WH):
        base = (6 - hj) * 8
        y = jnp.concatenate([u[:, dt * 104 + base : dt * 104 + base + 56] for dt in range(7)], axis=1)
        for tj in range(WT):
            z = y[:, (3 - tj) * 56 : (3 - tj) * 56 + ROWS]
            bias_ref[:, tj * 56 + hj * 8 : tj * 56 + hj * 8 + 8, :] = z.reshape(HEADS, 8, ROWS)


def table_pull(ds_ref):
    du = jnp.zeros((HEADS * 8, UPAD), f32)
    for hj in range(WH):
        dy = jnp.zeros((HEADS * 8, 392), f32)
        for tj in range(WT):
            z = ds_ref[:, tj * 56 + hj * 8 : tj * 56 + hj * 8 + 8, :].reshape(HEADS * 8, ROWS)
            parts = []
            if tj < 3:
                parts.append(jnp.zeros((HEADS * 8, (3 - tj) * 56), f32))
            parts.append(z)
            if tj > 0:
                parts.append(jnp.zeros((HEADS * 8, tj * 56), f32))
            dy = dy + (jnp.concatenate(parts, axis=1) if len(parts) > 1 else parts[0])
        parts = []
        at = 0
        for dt in range(7):
            start = dt * 104 + (6 - hj) * 8
            if start > at:
                parts.append(jnp.zeros((HEADS * 8, start - at), f32))
            parts.append(dy[:, dt * 56 : dt * 56 + 56])
            at = start + 56
        parts.append(jnp.zeros((HEADS * 8, UPAD - at), f32))
        du = du + jnp.concatenate(parts, axis=1)
    onehot = spread_onehot()
    hi = du.astype(bf16)
    lo = (du - hi.astype(f32)).astype(bf16)
    return dot(hi, onehot, NT) + dot(lo, onehot, NT)


def unsheared(sheared):
    sub = jnp.bitwise_and(lax.broadcasted_iota(jnp.int32, sheared.shape, 0), 7)
    total = jnp.zeros_like(sheared)
    for wj in range(WW):
        moved = pltpu.roll(sheared, TPAD - wj, 1) if wj else sheared
        total = jnp.where(sub == wj, moved, total)
    return [jnp.sum(total[8 * h : 8 * h + 8], axis=0, keepdims=True) for h in range(HEADS)]


def head_mask(hh):
    lane = lax.broadcasted_iota(jnp.int32, (1, 128), 1)
    return (lane >= hh * HD) & (lane < hh * HD + HD)


def masked(value, hh):
    return jnp.where(head_mask(hh), value, jnp.zeros_like(value))


def attention_forward(n_ref, wqkv_ref, bias_ref, qkv_ref, p_ref, ctxt_ref, ctx_ref):
    for c in range(3):
        cols = slice(c * D, c * D + D)
        qkv_ref[:, cols] = dot(n_ref[...], wqkv_ref[:, cols], NN).astype(bf16)
    for g in range(3):
        lanes = slice(g * 128, g * 128 + 128)
        q = qkv_ref[:, g * 128 : g * 128 + 128]
        k = qkv_ref[:, D + g * 128 : D + g * 128 + 128]
        v = qkv_ref[:, 2 * D + g * 128 : 2 * D + g * 128 + 128]
        vt = v.astype(f32).T.astype(bf16)
        for hh in range(4):
            h = 4 * g + hh
            s = dot(k, masked(q, hh), NT) * (HD**-0.5) + bias_ref[h]
            top = jnp.max(s, axis=0, keepdims=True)
            e = jnp.exp(s - top)
            p = (e * (1.0 / jnp.sum(e, axis=0, keepdims=True))).astype(bf16)
            p_ref[h] = p
            ctxt_ref[h * HD : h * HD + HD, :] = dot(vt[hh * HD : hh * HD + HD], p, NN)
        ctx_ref[:, lanes] = ctxt_ref[g * 128 : g * 128 + 128, :].T.astype(bf16)


def attention_backward(dctx, qkv_ref, p_ref, ds_ref, dqt_ref, dqkv_ref):
    for g in range(3):
        q = qkv_ref[:, g * 128 : g * 128 + 128]
        k = qkv_ref[:, D + g * 128 : D + g * 128 + 128]
        v = qkv_ref[:, 2 * D + g * 128 : 2 * D + g * 128 + 128]
        dc = dctx[:, g * 128 : g * 128 + 128]
        kt = k.astype(f32).T.astype(bf16)
        dk = jnp.zeros((ROWS, 128), f32)
        dv = jnp.zeros((ROWS, 128), f32)
        for hh in range(4):
            h = 4 * g + hh
            dch = masked(dc, hh)
            p = p_ref[h]
            p32 = p.astype(f32)
            dp = dot(v, dch, NT)
            delta = jnp.sum(p32 * dp, axis=0, keepdims=True)
            ds = p32 * (dp - delta)
            ds_ref[h] = ds.astype(ds_ref.dtype)
            dsb = ds.astype(bf16)
            dv = dv + dot(p, dch, NN)
            dk = dk + dot(dsb, masked(q, hh), NN)
            dqt_ref[h * HD : h * HD + HD, :] = dot(kt[hh * HD : hh * HD + HD], dsb, NN)
        dq = dqt_ref[g * 128 : g * 128 + 128, :].T
        dqkv_ref[:, g * 128 : g * 128 + 128] = (dq * (HD**-0.5)).astype(bf16)
        dqkv_ref[:, D + g * 128 : D + g * 128 + 128] = (dk * (HD**-0.5)).astype(bf16)
        dqkv_ref[:, 2 * D + g * 128 : 2 * D + g * 128 + 128] = dv.astype(bf16)


def expand_gelu(n2_ref, we_ref, e_ref, act_ref, slope_ref):
    for c in range(4):
        cols = slice(c * D, c * D + D)
        e_ref[...] = dot(n2_ref[...], we_ref[:, cols], NN)
        for i in row_steps():
            rows = slice(i, i + STEP)
            x = e_ref[rows, :]
            cdf = 0.5 + 0.5 * lax.erf(x * 0.7071067811865476)
            act_ref[rows, cols] = (x * cdf).astype(bf16)
            slope = cdf + x * (jnp.exp(x * x * -0.5) * 0.3989422804014327)
            slope_ref[rows, cols] = slope.astype(slope_ref.dtype)


def attention_and_feed(m, x):
    m.need("table", "wqkv")
    build_bias(m.table, m.bias, m.wide)
    norm_into(x, m.n1)
    attention_forward(m.n1, m.wqkv, m.bias, m.qkv, m.p, m.turned, m.ctx)
    m.need("wp", "we", "wc")
    m.ready("n1", "qkv", "p", "ctx")
    m.big[...] = dot(m.ctx[...], m.wp[...], NN)
    for i in row_steps():
        rows = slice(i, i + STEP)
        a = m.big[rows, :].astype(bf16).astype(f32)
        h = (x[rows, :].astype(f32) + a).astype(bf16)
        m.h[rows, :] = h
        m.n2[rows, :] = standardized(h.astype(f32))[0].astype(bf16)
    expand_gelu(m.n2, m.we, m.big, m.act, m.slope)
    m.ready("h", "n2", "act", "slope")


def first_forward(m):
    attention_and_feed(m, m.x)
    m.big[...] = dot(m.act[...], m.wc[...], NN)
    for i in row_steps():
        rows = slice(i, i + STEP)
        m.y[rows, :] = (m.h[rows, :].astype(f32) + m.big[rows, :]).astype(bf16)


def feed_backward(gy_ref, slope_ref, h_ref, we_ref, wc_ref, de_ref, big_ref, dh_ref):
    for c in range(4):
        cols = slice(c * D, c * D + D)
        big_ref[...] = dot(gy_ref[...], wc_ref[cols, :], NT)
        for i in row_steps():
            rows = slice(i, i + STEP)
            da = big_ref[rows, :].astype(bf16).astype(f32)
            de_ref[rows, cols] = (da * slope_ref[rows, cols].astype(f32)).astype(bf16)
    big_ref[...] = dot(de_ref[...], we_ref[...], NT)
    for i in row_steps():
        rows = slice(i, i + STEP)
        g = big_ref[rows, :].astype(bf16).astype(f32)
        back = norm_pull(h_ref[rows, :].astype(f32), g).astype(bf16)
        dh_ref[rows, :] = (gy_ref[rows, :].astype(f32) + back.astype(f32)).astype(bf16)


def attention_input_pull(x_ref, dqkv_ref, wqkv_ref, big_ref, dh_ref, dx_ref):
    big_ref[...] = dot(dqkv_ref[...], wqkv_ref[...], NT)
    for i in row_steps():
        rows = slice(i, i + STEP)
        g = big_ref[rows, :].astype(bf16).astype(f32)
        back = norm_pull(x_ref[rows, :].astype(f32), g).astype(bf16)
        dx_ref[rows, :] = (dh_ref[rows, :].astype(f32) + back.astype(f32)).astype(bf16)


def backward(m, x, gy, dx):
    m.need("wc", "slope", "we", "h")
    feed_backward(gy, m.slope, m.h, m.we, m.wc, m.de, m.big, m.dh)
    m.need("wp", "qkv", "p", "wqkv")
    m.dctx[...] = dot(m.dh[...], m.wp[...], NT).astype(bf16)
    attention_backward(m.dctx, m.qkv, m.p, m.ds, m.turned, m.dqkv)
    attention_input_pull(x, m.dqkv, m.wqkv, m.big, m.dh, dx)
    m.ready("ds", "dqkv", "de", "dh")


def second_whole(m):
    attention_and_feed(m, m.y)
    backward(m, m.y, m.up, m.gy)


def first_backward(m):
    backward(m, m.x, m.gy, m.dx)
    m.need("n1", "ctx", "n2", "act")
    weight_sums(m, m.ds)


def picker(per):
    count = D // per
    row = lax.broadcasted_iota(jnp.int32, (D, 1), 0)
    r = jnp.zeros((D, 1), jnp.int32)
    for step in range(1, per):
        r = r + jnp.where(row >= step * count, 1, 0)
    target = (row - r * count) * per + r
    col = lax.broadcasted_iota(jnp.int32, (D, D), 1)
    return jnp.where(col == target, 1.0, 0.0).astype(bf16)


def weights_kernel(m):
    m.passed[...] = m.carried[...]
    m.need("n1", "dqkv", "ctx", "dh", "n2", "de", "act", "ds")
    for h in range(HEADS):
        m.wide[h] = m.ds[h].astype(f32)
    weight_sums(m, m.wide)


def weight_sums(m, ds):
    f_ref = m.f
    pick = picker(3)

    def place(first, x, g_ref, pick, per, owner):
        width = g_ref.shape[1] // 128
        count = D // per
        xt = dot(pick, x, NT).astype(bf16)
        for c in range(0, width, 3):
            dw = dot(xt, g_ref[:, c * 128 : c * 128 + 384], NN)
            for r in range(per):
                for k in range(3):
                    at = owner * CHUNK + first + r * width + c + k
                    f_ref[pl.ds(at, count, stride=CHUNK), :] = dw[r * count : r * count + count, k * 128 : k * 128 + 128]

    place(0, m.n1[...], m.dqkv, pick, 3, 0)
    place(27, m.ctx[...], m.dh, pick, 3, 0)
    place(36, m.n2[...], m.de, pick, 3, 0)
    pick = picker(12)
    for b in range(4):
        place(72, m.act[:, b * D : b * D + D], m.gy, pick, 12, b * 32)
    lines = unsheared(table_pull(ds))
    zero = jnp.zeros((128, 128), f32)
    for j in range(108, CHUNK):
        f_ref[pl.ds(j, 128, stride=CHUNK), :] = zero
    for h in range(HEADS):
        for c in range(10):
            at = (h * 10 + c) * CHUNK + 108
            f_ref[at : at + 1, :] = lines[h][:, c * 128 : c * 128 + 128]
    mine = m.mine[0]

    def half(ref, offset):
        def step(i, carry):
            to = pl.ds(pl.multiple_of(i * CHUNK, CHUNK), CHUNK)
            ref[to, :] = f_ref[pl.ds(pl.multiple_of((2 * i + offset) * CHUNK, CHUNK), CHUNK), :].astype(bf16)
            return carry

        lax.fori_loop(0, 64, step, 0, unroll=8)

    half(m.give, 1 - mine)
    m.ready("give")
    half(m.keep, mine)
    m.ready("keep")


SQUARE = (HEADS, ROWS, ROWS)


def scr(shape, dtype):
    return pltpu.VMEM(shape, dtype)


def rows(width, space):
    return (ROWS, width), bf16, space


def run_first_forward(x, table, weights):
    return launch(
        first_forward,
        {"x": (x, "near"), "table": (table, "far")} | weights,
        {
            "n1": rows(D, "far"), "qkv": rows(3 * D, "far"), "p": (SQUARE, bf16, "far"), "ctx": rows(D, "far"),
            "h": rows(D, "far"), "n2": rows(D, "far"), "act": rows(FF, "far"), "slope": rows(FF, "far"),
            "y": rows(D, "near"),
        },
        {
            "bias": scr(SQUARE, f32), "turned": scr((D, ROWS), f32), "big": scr((ROWS, D), f32),
            "wide": scr((16, TPAD), f32),
        },
    )


def run_second(y, up, table, weights):
    return launch(
        second_whole,
        {"y": (y, "near"), "up": (up, "near"), "table": (table, "near")} | weights,
        {
            "n1": rows(D, "far"), "ctx": rows(D, "far"), "n2": rows(D, "far"), "act": rows(FF, "far"),
            "dqkv": rows(3 * D, "far"), "dh": rows(D, "far"), "de": rows(FF, "far"), "ds": (SQUARE, bf16, "far"),
            "gy": rows(D, "near"),
        },
        {
            "bias": scr(SQUARE, f32), "wide": scr((16, TPAD), f32),
            "qkv": scr((ROWS, 3 * D), bf16), "p": scr(SQUARE, bf16), "turned": scr((D, ROWS), f32),
            "h": scr((ROWS, D), bf16), "slope": scr((ROWS, FF), bf16), "dctx": scr((ROWS, D), bf16),
            "big": scr((ROWS, D), f32),
        },
    )


HALF = ((64 * CHUNK, 128), bf16, "far")


def run_first_backward(mine, gy, x, kept, weights):
    return launch(
        first_backward,
        {"mine": (mine, "flag"), "gy": (gy, "near"), "x": (x, "near"), "wc": (weights["wc"][0], "near")}
        | {"slope": (kept["slope"], "near"), "we": (weights["we"][0], "near"), "h": (kept["h"], "near")}
        | {"wp": weights["wp"]}
        | {"qkv": (kept["qkv"], "far"), "p": (kept["p"], "far"), "wqkv": weights["wqkv"]}
        | {name: (kept[name], "far") for name in ("n1", "ctx", "n2", "act")},
        {"dx": rows(D, "near"), "keep": HALF, "give": HALF},
        {
            "turned": scr((D, ROWS), f32), "dctx": scr((ROWS, D), bf16), "big": scr((ROWS, D), f32),
            "dqkv": scr((ROWS, 3 * D), bf16), "dh": scr((ROWS, D), bf16), "de": scr((ROWS, FF), bf16),
            "ds": scr(SQUARE, f32), "f": scr((128 * CHUNK, 128), f32),
        },
    )


def run_weights(mine, sums, gy, carried):
    return launch(
        weights_kernel,
        {"mine": (mine, "flag"), "gy": (gy, "near"), "carried": (carried, "near")}
        | {name: (sums[name], "far") for name in ("n1", "ctx", "n2", "act", "dqkv", "dh", "de", "ds")},
        {"keep": HALF, "give": HALF, "passed": (carried.shape, carried.dtype, "near")},
        {"f": scr((128 * CHUNK, 128), f32), "wide": scr(SQUARE, f32)},
    )


PIECES = 4


def merge_kernel(m):
    per = 64 // PIECES
    for piece in range(PIECES):
        m.need(f"keep_one{piece}", f"keep_two{piece}")
        keeps = m.__dict__[f"keep_one{piece}"], m.__dict__[f"keep_two{piece}"]

        def step(j, carry):
            chunk = pl.ds(pl.multiple_of((piece * per + j) * CHUNK, CHUNK), CHUNK)
            own = pl.ds(pl.multiple_of(j * CHUNK, CHUNK), CHUNK)
            for b, (kept, arrived) in enumerate(zip(keeps, (m.arrived_one, m.arrived_two))):
                total = kept[own, :].astype(f32) + arrived[chunk, :].astype(f32)
                to = pl.ds(pl.multiple_of((2 * j + b) * CHUNK, CHUNK), CHUNK)
                m.__dict__[f"both{piece}"][to, :] = total.astype(bf16)
            return carry

        lax.fori_loop(0, per, step, 0, unroll=4)
        m.ready(f"both{piece}")


def run_merge(keep_one, keep_two, arrived_one, arrived_two):
    ins = {"keep_two": keep_two, "keep_one": keep_one}
    near = {"arrived_one": arrived_one, "arrived_two": arrived_two}
    both = launch(
        merge_kernel,
        {name: (array, "parts") for name, array in ins.items()} | {name: (array, "near") for name, array in near.items()},
        {"both": ((128 * CHUNK, 128), bf16, "parts")},
    )["both"]
    return both.reshape(64, 2 * CHUNK, 128)


def finish_kernel(m):
    per = 64 // PIECES
    total = None
    for piece in range(PIECES):
        m.need(f"spread{piece}")
        part = m.__dict__[f"spread{piece}"]

        def step(i, carry):
            return carry + part[i].astype(f32)

        total = lax.fori_loop(0, per, step, total if piece else jnp.zeros((2 * CHUNK, 128), f32), unroll=2)
    m.total[...] = total
    for b in range(2):
        at = b * CHUNK
        for name, first, count, width in (("qkv", 0, 3, 9), ("proj", 27, 3, 3), ("expand", 36, 3, 12), ("contract", 72, 12, 3)):
            target = m.__dict__[f"{name}_{b}"]
            for r in range(count):
                for c in range(width):
                    row = at + first + r * width + c
                    target[r : r + 1, c * 128 : c * 128 + 128] = m.total[row : row + 1, :]


def lines_kernel(spread, lines_ref, near_ref, sems):
    copies = [
        pltpu.make_async_copy(spread.at[:, pl.ds(b * CHUNK + 96, 16), :], near_ref.at[b], sems.at[b]) for b in range(2)
    ]
    for copy in copies:
        copy.start()
    for b, copy in enumerate(copies):
        copy.wait()
        total = jnp.zeros((16, 128), f32)
        for i in range(64):
            total = total + near_ref[b, i].astype(f32)
        lines_ref[:, b, :] = jnp.broadcast_to(total[12:13], (128, 128))


def run_lines(spread):
    return pl.pallas_call(
        lines_kernel,
        out_shape=jax.ShapeDtypeStruct((128, 2, 128), f32),
        in_specs=[pl.BlockSpec(memory_space=pltpu.HBM)],
        out_specs=pl.BlockSpec(memory_space=pltpu.VMEM),
        scratch_shapes=[pltpu.VMEM((2, 64, 16, 128), bf16), pltpu.SemaphoreType.DMA((2,))],
        compiler_params=pltpu.CompilerParams(vmem_limit_bytes=VMEM_LIMIT),
    )(pltpu.with_memory_space_constraint(spread, pltpu.HBM))


def run_finish(spread):
    outs = {}
    for b in range(2):
        outs |= {f"qkv_{b}": ((3, 3 * D), f32, "near"), f"proj_{b}": ((3, D), f32, "near")}
        outs |= {f"expand_{b}": ((3, FF), f32, "near"), f"contract_{b}": ((12, D), f32, "near")}
    return launch(
        finish_kernel,
        {"spread": (spread, "parts")},
        outs,
        {"total": pltpu.VMEM((2 * CHUNK, 128), f32)},
    )


def passed_along(block, axis, distance):
    devices = range(lax.axis_size(axis))
    route = [((i - distance) % len(devices), i) for i in devices]
    return lax.ppermute(block, axis, route)


def edge_of(grid, dim, width, direction):
    extent = grid.shape[dim]
    if direction < 0:
        return lax.slice_in_dim(grid, 0, width, axis=dim)
    return lax.slice_in_dim(grid, extent - width, extent, axis=dim)


def rejoin(grid, dim, width, direction, arrived):
    extent = grid.shape[dim]
    if direction < 0:
        return jnp.concatenate([lax.slice_in_dim(grid, width, extent, axis=dim), arrived], axis=dim)
    return jnp.concatenate([arrived, lax.slice_in_dim(grid, 0, extent - width, axis=dim)], axis=dim)


def rolled_along(grid, dim, direction):
    width = (WT // 2, WH // 2, WW // 2)[dim]
    at = grid.ndim - 4 + dim
    moved = passed_along(edge_of(grid, at, width, direction), AXES[dim], direction)
    return rejoin(grid, at, width, direction, moved)


def rolled_twice(grid, direction):
    first = grid.ndim - 4
    sizes = [lax.axis_size(axis) for axis in AXES[:2]]
    parts = {}
    for bt in range(2):
        for bh in range(2):
            part = grid
            for at, width, moves in ((first, WT // 2, bt), (first + 1, WH // 2, bh)):
                extent = part.shape[at]
                if moves:
                    part = edge_of(part, at, width, direction)
                elif direction < 0:
                    part = lax.slice_in_dim(part, width, extent, axis=at)
                else:
                    part = lax.slice_in_dim(part, 0, extent - width, axis=at)
            if bt or bh:
                route = [
                    (t * sizes[1] + h, (t + bt * direction) % sizes[0] * sizes[1] + (h + bh * direction) % sizes[1])
                    for t in range(sizes[0])
                    for h in range(sizes[1])
                ]
                part = lax.ppermute(part, AXES[:2], route)
            parts[bt, bh] = part
    order = (0, 1) if direction < 0 else (1, 0)
    halves = [jnp.concatenate([parts[bt, bh] for bh in order], axis=first + 1) for bt in order]
    return jnp.concatenate(halves, axis=first)


def to_rows(grid):
    return jnp.pad(grid, ((0, 0), (0, 0), (0, 1), (0, 0))).reshape(ROWS, D)


def to_grid(flat):
    return flat.reshape(WT, WH, PITCH, D)[:, :, :WW]


def swapped(block):
    return lax.ppermute(block, "wa", [(i, i ^ 1) for i in range(lax.axis_size("wa"))])


def exchanged(both):
    groups = [[i for i in range(128) if i % 2 == side] for side in range(2)]
    return lax.all_to_all(both, AXES, 0, 0, axis_index_groups=groups, tiled=True)


def body(
    tokens, upstream, qkv_one, proj_one, table_one, expand_one, contract_one,
    qkv_two, proj_two, table_two, expand_two, contract_two,
):
    mine = (lax.axis_index("wa") % 2).astype(jnp.int32).reshape(1)
    x = to_rows(tokens)

    def far(wqkv, wp, we, wc):
        return {"wqkv": (wqkv, "far"), "wp": (wp, "far"), "we": (we, "far"), "wc": (wc, "far")}

    weights_one = far(qkv_one, proj_one, expand_one, contract_one)
    weights_two = far(qkv_two, proj_two, expand_two, contract_two)
    one = run_first_forward(x, table_one, weights_one)
    both = jnp.stack([to_grid(one["y"]), upstream])
    both = rolled_along(rolled_twice(both, -1), 2, -1)
    rolled, up = to_rows(both[0]), to_rows(both[1])
    two = run_second(rolled, up, table_two, {name: (w, "near") for name, (w, _) in weights_two.items()})
    gy = rolled_twice(to_grid(two["gy"]), 1)
    sent = passed_along(edge_of(gy, 2, WW // 2, 1), AXES[2], 1)
    sums_two = run_weights(mine, two, up, to_rows(gy))
    gy = to_rows(rejoin(to_grid(sums_two["passed"]), 2, WW // 2, 1, sent))
    arrived_two = swapped(sums_two["give"])
    sums_one = run_first_backward(mine, gy, x, one, weights_one)
    dx = sums_one["dx"]
    spread = exchanged(
        run_merge(sums_one["keep"], sums_two["keep"], swapped(sums_one["give"]), arrived_two)
    )
    tables = lax.all_to_all(run_lines(spread), AXES, 0, 0, tiled=True)
    done = run_finish(spread)

    def table_of(which):
        return tables[:120, which].reshape(HEADS, TPAD)[:, :TABLE]

    g1, g2 = ([done[f"{name}_{b}"] for name in ("qkv", "proj", "expand", "contract")] for b in range(2))
    return (
        to_grid(dx), g1[0], g1[1], table_of(0), g1[2], g1[3],
        g2[0], g2[1], table_of(1), g2[2], g2[3],
    )


def solution(mesh):
    grid = P("ta", "ha", "wa", None)
    rows_split = P(AXES, None)
    return jax.shard_map(
        body,
        mesh=mesh,
        in_specs=(grid, grid) + (P(),) * 10,
        out_specs=(
            grid, rows_split, rows_split, P(), rows_split, rows_split,
            rows_split, rows_split, P(), rows_split, rows_split,
        ),
        check_vma=False,
    )
```

```python
import jax
import jax.numpy as jnp
from jax import lax
from jax.experimental import pallas as pl
from jax.experimental.pallas import tpu as pltpu
from jax.sharding import PartitionSpec as P

HEADS = 12
WT = 4
WH = 7
WW = 7
PITCH = 8
ROWS = WT * WH * PITCH
D = 384
FF = 1536
HD = 32
TABLE = 1183
TPAD = 1280
UPAD = 768
STEP = 32
CHUNK = 112
VMEM_LIMIT = 32 * 1024 * 1024
epsilon = 1e-05
f32 = jnp.float32
bf16 = jnp.bfloat16
NN = ((1,), (0,))
NT = ((1,), (1,))
AXES = ("ta", "ha", "wa")


def dot(a, b, dims):
    return lax.dot_general(a, b, (dims, ((), ())), preferred_element_type=f32)


class Held:
    def __init__(self, refs, incoming, outgoing):
        self.__dict__.update(refs)
        self.incoming = dict(incoming)
        self.outgoing = dict(outgoing)

    def need(self, *names):
        for name in names:
            if name in self.incoming:
                self.incoming.pop(name).wait()

    def ready(self, *names):
        for name in names:
            if name in self.outgoing:
                self.outgoing.pop(name).start()


def launch(kernel, ins, outs, scratch=()):
    places = {"parts": pltpu.HBM, "far": pltpu.HBM, "near": pltpu.VMEM, "flag": pltpu.SMEM, "pass": pltpu.HBM}
    passed = [n for n, (_, space) in ins.items() if space == "pass"]
    outs = dict(outs) | {n: (ins[n][0].shape, ins[n][0].dtype, "pass") for n in passed}
    scratch = dict(scratch)
    buffers = {}

    def copied(named, space, shape, dtype):
        cuts = {"far": 1, "parts": PIECES}.get(space, 0)
        size = shape[0] // max(cuts, 1)
        names = [named] if cuts == 1 else [f"{named}{i}" for i in range(cuts)]
        for name in names:
            buffers[name] = pltpu.VMEM((size,) + tuple(shape[1:]), dtype)
        return {name: (named, i * size, size) for i, name in enumerate(names)}

    far_ins, far_outs = {}, {}
    for n, (array, space) in ins.items():
        far_ins |= copied(n, space, array.shape, array.dtype)
    for n, (shape, dtype, space) in outs.items():
        far_outs |= copied(n, space, shape, dtype)

    def wrapped(*refs):
        named = dict(zip(list(ins) + list(outs), refs))
        rest = refs[len(ins) + len(outs) :]
        near = dict(zip(list(scratch) + list(buffers), rest))
        sems = rest[-1]
        incoming, outgoing = {}, {}
        for i, (n, (whole, first, size)) in enumerate(far_ins.items()):
            incoming[n] = pltpu.make_async_copy(named[whole].at[pl.ds(first, size)], near[n], sems.at[i])
            incoming[n].start()
        for i, (n, (whole, first, size)) in enumerate(far_outs.items()):
            cut = named[whole].at[pl.ds(first, size)]
            outgoing[n] = pltpu.make_async_copy(near[n], cut, sems.at[len(far_ins) + i])
        kernel(Held({**named, **near}, incoming, outgoing))
        for n in far_outs:
            outgoing[n].wait()

    results = pl.pallas_call(
        wrapped,
        out_shape=[
            pltpu.HBM(shape, dtype) if space in ("far", "parts", "pass") else jax.ShapeDtypeStruct(shape, dtype)
            for shape, dtype, space in outs.values()
        ],
        in_specs=[pl.BlockSpec(memory_space=places[space]) for _, space in ins.values()],
        out_specs=[pl.BlockSpec(memory_space=places[space]) for _, _, space in outs.values()],
        input_output_aliases={list(ins).index(n): list(outs).index(n) for n in passed},
        scratch_shapes=list(scratch.values())
        + list(buffers.values())
        + [pltpu.SemaphoreType.DMA((max(1, len(far_ins) + len(far_outs)),))],
        compiler_params=pltpu.CompilerParams(vmem_limit_bytes=VMEM_LIMIT),
    )(
        *[
            pltpu.with_memory_space_constraint(array, pltpu.HBM) if space in ("far", "parts", "pass") else array
            for array, space in ins.values()
        ]
    )
    return dict(zip(outs, results))


def row_steps():
    return range(0, ROWS, STEP)


def standardized(x):
    average = jnp.sum(x, axis=-1, keepdims=True) * (1.0 / D)
    centred = x - average
    spread = jnp.sum(centred * centred, axis=-1, keepdims=True) * (1.0 / D)
    scale = lax.rsqrt(spread + epsilon)
    return centred * scale, scale


def norm_pull(x, grad):
    unit, scale = standardized(x)
    mean_grad = jnp.sum(grad, axis=-1, keepdims=True) * (1.0 / D)
    mean_both = jnp.sum(grad * unit, axis=-1, keepdims=True) * (1.0 / D)
    return scale * (grad - mean_grad - unit * mean_both)


def norm_into(src, dst):
    for i in row_steps():
        rows = pl.ds(i, STEP)
        dst[rows, :] = standardized(src[rows, :].astype(f32))[0].astype(bf16)


def split3(x):
    hi = x.astype(bf16)
    rest = x - hi.astype(f32)
    mid = rest.astype(bf16)
    return hi, mid, (rest - mid.astype(f32)).astype(bf16)


def spread_onehot():
    col = lax.broadcasted_iota(jnp.int32, (1, UPAD), 1)
    group = lax.shift_right_logical(col, 3)
    w = jnp.bitwise_and(col, 7)
    valid = (w < WW) & (group < 91)
    target = jnp.where(valid, group * 13 + w + 6, -1)
    row = lax.broadcasted_iota(jnp.int32, (TPAD, UPAD), 0)
    return jnp.where(row == target, 1.0, 0.0).astype(bf16)


def build_bias(table_ref, bias_ref, wide_ref):
    wide_ref[...] = jnp.zeros_like(wide_ref)
    wide_ref[:HEADS, :TABLE] = table_ref[...]
    sheared = []
    for h in range(HEADS):
        line = jnp.broadcast_to(wide_ref[h : h + 1, :], (8, TPAD))
        sheared.append(pltpu.roll(line, 0, 1, stride=1, stride_axis=0))
    sheared = jnp.concatenate(sheared, axis=0)
    onehot = spread_onehot()
    hi, mid, lo = split3(sheared)
    u = dot(hi, onehot, NN) + dot(mid, onehot, NN) + dot(lo, onehot, NN)
    sub = lax.broadcasted_iota(jnp.int32, u.shape, 0)
    u = jnp.where(jnp.bitwise_and(sub, 7) == 7, -1e30, u)
    for hj in range(WH):
        base = (6 - hj) * 8
        y = jnp.concatenate([u[:, dt * 104 + base : dt * 104 + base + 56] for dt in range(7)], axis=1)
        for tj in range(WT):
            z = y[:, (3 - tj) * 56 : (3 - tj) * 56 + ROWS]
            bias_ref[:, tj * 56 + hj * 8 : tj * 56 + hj * 8 + 8, :] = z.reshape(HEADS, 8, ROWS)


def table_pull(ds_ref):
    du = jnp.zeros((HEADS * 8, UPAD), f32)
    for hj in range(WH):
        dy = jnp.zeros((HEADS * 8, 392), f32)
        for tj in range(WT):
            z = ds_ref[:, tj * 56 + hj * 8 : tj * 56 + hj * 8 + 8, :].reshape(HEADS * 8, ROWS)
            parts = []
            if tj < 3:
                parts.append(jnp.zeros((HEADS * 8, (3 - tj) * 56), f32))
            parts.append(z)
            if tj > 0:
                parts.append(jnp.zeros((HEADS * 8, tj * 56), f32))
            dy = dy + (jnp.concatenate(parts, axis=1) if len(parts) > 1 else parts[0])
        parts = []
        at = 0
        for dt in range(7):
            start = dt * 104 + (6 - hj) * 8
            if start > at:
                parts.append(jnp.zeros((HEADS * 8, start - at), f32))
            parts.append(dy[:, dt * 56 : dt * 56 + 56])
            at = start + 56
        parts.append(jnp.zeros((HEADS * 8, UPAD - at), f32))
        du = du + jnp.concatenate(parts, axis=1)
    onehot = spread_onehot()
    hi = du.astype(bf16)
    lo = (du - hi.astype(f32)).astype(bf16)
    return dot(hi, onehot, NT) + dot(lo, onehot, NT)


def unsheared(sheared):
    sub = jnp.bitwise_and(lax.broadcasted_iota(jnp.int32, sheared.shape, 0), 7)
    total = jnp.zeros_like(sheared)
    for wj in range(WW):
        moved = pltpu.roll(sheared, TPAD - wj, 1) if wj else sheared
        total = jnp.where(sub == wj, moved, total)
    return [jnp.sum(total[8 * h : 8 * h + 8], axis=0, keepdims=True) for h in range(HEADS)]


def head_mask(hh):
    lane = lax.broadcasted_iota(jnp.int32, (1, 128), 1)
    return (lane >= hh * HD) & (lane < hh * HD + HD)


def masked(value, hh):
    return jnp.where(head_mask(hh), value, jnp.zeros_like(value))


def attention_forward(n_ref, wqkv_ref, bias_ref, qkv_ref, p_ref, ctxt_ref, ctx_ref):
    for c in range(3):
        cols = slice(c * D, c * D + D)
        qkv_ref[:, cols] = dot(n_ref[...], wqkv_ref[:, cols], NN).astype(bf16)
    for g in range(3):
        lanes = slice(g * 128, g * 128 + 128)
        q = qkv_ref[:, g * 128 : g * 128 + 128]
        k = qkv_ref[:, D + g * 128 : D + g * 128 + 128]
        v = qkv_ref[:, 2 * D + g * 128 : 2 * D + g * 128 + 128]
        vt = v.astype(f32).T.astype(bf16)
        for hh in range(4):
            h = 4 * g + hh
            s = dot(k, masked(q, hh), NT) * (HD**-0.5) + bias_ref[h]
            top = jnp.max(s, axis=0, keepdims=True)
            e = jnp.exp(s - top)
            p = (e * (1.0 / jnp.sum(e, axis=0, keepdims=True))).astype(bf16)
            p_ref[h] = p
            ctxt_ref[h * HD : h * HD + HD, :] = dot(vt[hh * HD : hh * HD + HD], p, NN)
        ctx_ref[:, lanes] = ctxt_ref[g * 128 : g * 128 + 128, :].T.astype(bf16)


def attention_backward(dctx, qkv_ref, p_ref, ds_ref, dqt_ref, dqkv_ref):
    for g in range(3):
        q = qkv_ref[:, g * 128 : g * 128 + 128]
        k = qkv_ref[:, D + g * 128 : D + g * 128 + 128]
        v = qkv_ref[:, 2 * D + g * 128 : 2 * D + g * 128 + 128]
        dc = dctx[:, g * 128 : g * 128 + 128]
        kt = k.astype(f32).T.astype(bf16)
        dk = jnp.zeros((ROWS, 128), f32)
        dv = jnp.zeros((ROWS, 128), f32)
        for hh in range(4):
            h = 4 * g + hh
            dch = masked(dc, hh)
            p = p_ref[h]
            p32 = p.astype(f32)
            dp = dot(v, dch, NT)
            delta = jnp.sum(p32 * dp, axis=0, keepdims=True)
            ds = p32 * (dp - delta)
            ds_ref[h] = ds.astype(ds_ref.dtype)
            dsb = ds.astype(bf16)
            dv = dv + dot(p, dch, NN)
            dk = dk + dot(dsb, masked(q, hh), NN)
            dqt_ref[h * HD : h * HD + HD, :] = dot(kt[hh * HD : hh * HD + HD], dsb, NN)
        dq = dqt_ref[g * 128 : g * 128 + 128, :].T
        dqkv_ref[:, g * 128 : g * 128 + 128] = (dq * (HD**-0.5)).astype(bf16)
        dqkv_ref[:, D + g * 128 : D + g * 128 + 128] = (dk * (HD**-0.5)).astype(bf16)
        dqkv_ref[:, 2 * D + g * 128 : 2 * D + g * 128 + 128] = dv.astype(bf16)


def expand_gelu(n2_ref, we_ref, e_ref, act_ref, slope_ref):
    for c in range(4):
        cols = slice(c * D, c * D + D)
        e_ref[...] = dot(n2_ref[...], we_ref[:, cols], NN)
        for i in row_steps():
            rows = slice(i, i + STEP)
            x = e_ref[rows, :]
            cdf = 0.5 + 0.5 * lax.erf(x * 0.7071067811865476)
            act_ref[rows, cols] = (x * cdf).astype(bf16)
            slope = cdf + x * (jnp.exp(x * x * -0.5) * 0.3989422804014327)
            slope_ref[rows, cols] = slope.astype(slope_ref.dtype)


def attention_and_feed(m, x):
    m.need("table", "wqkv")
    build_bias(m.table, m.bias, m.wide)
    norm_into(x, m.n1)
    attention_forward(m.n1, m.wqkv, m.bias, m.qkv, m.p, m.turned, m.ctx)
    m.need("wp", "we", "wc")
    m.ready("n1", "qkv", "p", "ctx")
    m.big[...] = dot(m.ctx[...], m.wp[...], NN)
    for i in row_steps():
        rows = slice(i, i + STEP)
        a = m.big[rows, :].astype(bf16).astype(f32)
        h = (x[rows, :].astype(f32) + a).astype(bf16)
        m.h[rows, :] = h
        m.n2[rows, :] = standardized(h.astype(f32))[0].astype(bf16)
    expand_gelu(m.n2, m.we, m.big, m.act, m.slope)
    m.ready("h", "n2", "act", "slope")


def first_forward(m):
    attention_and_feed(m, m.x)
    m.big[...] = dot(m.act[...], m.wc[...], NN)
    for i in row_steps():
        rows = slice(i, i + STEP)
        m.y[rows, :] = (m.h[rows, :].astype(f32) + m.big[rows, :]).astype(bf16)


def feed_backward(gy_ref, slope_ref, h_ref, we_ref, wc_ref, de_ref, big_ref, dh_ref):
    for c in range(4):
        cols = slice(c * D, c * D + D)
        big_ref[...] = dot(gy_ref[...], wc_ref[cols, :], NT)
        for i in row_steps():
            rows = slice(i, i + STEP)
            da = big_ref[rows, :].astype(bf16).astype(f32)
            de_ref[rows, cols] = (da * slope_ref[rows, cols].astype(f32)).astype(bf16)
    big_ref[...] = dot(de_ref[...], we_ref[...], NT)
    for i in row_steps():
        rows = slice(i, i + STEP)
        g = big_ref[rows, :].astype(bf16).astype(f32)
        back = norm_pull(h_ref[rows, :].astype(f32), g).astype(bf16)
        dh_ref[rows, :] = (gy_ref[rows, :].astype(f32) + back.astype(f32)).astype(bf16)


def attention_input_pull(x_ref, dqkv_ref, wqkv_ref, big_ref, dh_ref, dx_ref):
    big_ref[...] = dot(dqkv_ref[...], wqkv_ref[...], NT)
    for i in row_steps():
        rows = slice(i, i + STEP)
        g = big_ref[rows, :].astype(bf16).astype(f32)
        back = norm_pull(x_ref[rows, :].astype(f32), g).astype(bf16)
        dx_ref[rows, :] = (dh_ref[rows, :].astype(f32) + back.astype(f32)).astype(bf16)


def backward(m, x, gy, dx):
    m.need("wc", "slope", "we", "h")
    feed_backward(gy, m.slope, m.h, m.we, m.wc, m.de, m.big, m.dh)
    m.need("wp", "qkv", "p", "wqkv")
    m.dctx[...] = dot(m.dh[...], m.wp[...], NT).astype(bf16)
    attention_backward(m.dctx, m.qkv, m.p, m.ds, m.turned, m.dqkv)
    attention_input_pull(x, m.dqkv, m.wqkv, m.big, m.dh, dx)
    m.ready("ds", "dqkv", "de", "dh")


def second_whole(m):
    attention_and_feed(m, m.y)
    backward(m, m.y, m.up, m.gy)


def first_backward(m):
    backward(m, m.x, m.gy, m.dx)
    m.need("n1", "ctx", "n2", "act")
    weight_sums(m, m.ds)


def picker(per):
    count = D // per
    row = lax.broadcasted_iota(jnp.int32, (D, 1), 0)
    r = jnp.zeros((D, 1), jnp.int32)
    for step in range(1, per):
        r = r + jnp.where(row >= step * count, 1, 0)
    target = (row - r * count) * per + r
    col = lax.broadcasted_iota(jnp.int32, (D, D), 1)
    return jnp.where(col == target, 1.0, 0.0).astype(bf16)


def weights_kernel(m):
    m.passed[...] = m.carried[...]
    m.need("n1", "dqkv", "ctx", "dh", "n2", "de", "act", "ds")
    for h in range(HEADS):
        m.wide[h] = m.ds[h].astype(f32)
    weight_sums(m, m.wide)


def weight_sums(m, ds):
    f_ref = m.f
    pick = picker(3)

    def place(first, x, g_ref, pick, per, owner):
        width = g_ref.shape[1] // 128
        count = D // per
        xt = dot(pick, x, NT).astype(bf16)
        for c in range(0, width, 3):
            dw = dot(xt, g_ref[:, c * 128 : c * 128 + 384], NN)
            for r in range(per):
                for k in range(3):
                    at = owner * CHUNK + first + r * width + c + k
                    f_ref[pl.ds(at, count, stride=CHUNK), :] = dw[r * count : r * count + count, k * 128 : k * 128 + 128]

    place(0, m.n1[...], m.dqkv, pick, 3, 0)
    place(27, m.ctx[...], m.dh, pick, 3, 0)
    place(36, m.n2[...], m.de, pick, 3, 0)
    pick = picker(12)
    for b in range(4):
        place(72, m.act[:, b * D : b * D + D], m.gy, pick, 12, b * 32)
    lines = unsheared(table_pull(ds))
    zero = jnp.zeros((128, 128), f32)
    for j in range(108, CHUNK):
        f_ref[pl.ds(j, 128, stride=CHUNK), :] = zero
    for h in range(HEADS):
        for c in range(10):
            at = (h * 10 + c) * CHUNK + 108
            f_ref[at : at + 1, :] = lines[h][:, c * 128 : c * 128 + 128]
    mine = m.mine[0]

    def half(ref, offset):
        def step(i, carry):
            to = pl.ds(pl.multiple_of(i * CHUNK, CHUNK), CHUNK)
            ref[to, :] = f_ref[pl.ds(pl.multiple_of((2 * i + offset) * CHUNK, CHUNK), CHUNK), :].astype(bf16)
            return carry

        lax.fori_loop(0, 64, step, 0, unroll=8)

    half(m.give, 1 - mine)
    m.ready("give")
    half(m.keep, mine)
    m.ready("keep")


SQUARE = (HEADS, ROWS, ROWS)


def scr(shape, dtype):
    return pltpu.VMEM(shape, dtype)


def rows(width, space):
    return (ROWS, width), bf16, space


def run_first_forward(x, table, weights):
    return launch(
        first_forward,
        {"x": (x, "near"), "table": (table, "far")} | weights,
        {
            "n1": rows(D, "far"), "qkv": rows(3 * D, "far"), "p": (SQUARE, bf16, "far"), "ctx": rows(D, "far"),
            "h": rows(D, "far"), "n2": rows(D, "far"), "act": rows(FF, "far"), "slope": rows(FF, "far"),
            "y": rows(D, "near"),
        },
        {
            "bias": scr(SQUARE, f32), "turned": scr((D, ROWS), f32), "big": scr((ROWS, D), f32),
            "wide": scr((16, TPAD), f32),
        },
    )


def run_second(y, up, table, weights):
    return launch(
        second_whole,
        {"y": (y, "near"), "up": (up, "near"), "table": (table, "near")} | weights,
        {
            "n1": rows(D, "far"), "ctx": rows(D, "far"), "n2": rows(D, "far"), "act": rows(FF, "far"),
            "dqkv": rows(3 * D, "far"), "dh": rows(D, "far"), "de": rows(FF, "far"), "ds": (SQUARE, bf16, "far"),
            "gy": rows(D, "near"),
        },
        {
            "bias": scr(SQUARE, f32), "wide": scr((16, TPAD), f32),
            "qkv": scr((ROWS, 3 * D), bf16), "p": scr(SQUARE, bf16), "turned": scr((D, ROWS), f32),
            "h": scr((ROWS, D), bf16), "slope": scr((ROWS, FF), bf16), "dctx": scr((ROWS, D), bf16),
            "big": scr((ROWS, D), f32),
        },
    )


HALF = ((64 * CHUNK, 128), bf16, "far")


def run_first_backward(mine, gy, x, kept, weights):
    return launch(
        first_backward,
        {"mine": (mine, "flag"), "gy": (gy, "near"), "x": (x, "near"), "wc": (weights["wc"][0], "near")}
        | {"slope": (kept["slope"], "near"), "we": (weights["we"][0], "near"), "h": (kept["h"], "near")}
        | {"wp": (weights["wp"][0], "near"), "wqkv": (weights["wqkv"][0], "near")}
        | {"qkv": (kept["qkv"], "near"), "p": (kept["p"], "near")}
        | {name: (kept[name], "far") for name in ("n1", "ctx", "n2", "act")},
        {"dx": rows(D, "near"), "keep": HALF, "give": HALF},
        {
            "turned": scr((D, ROWS), f32), "dctx": scr((ROWS, D), bf16), "big": scr((ROWS, D), f32),
            "dqkv": scr((ROWS, 3 * D), bf16), "dh": scr((ROWS, D), bf16), "de": scr((ROWS, FF), bf16),
            "ds": scr(SQUARE, f32), "f": scr((128 * CHUNK, 128), f32),
        },
    )


def run_weights(mine, sums, gy, carried):
    return launch(
        weights_kernel,
        {"mine": (mine, "flag"), "gy": (gy, "near"), "carried": (carried, "near")}
        | {name: (sums[name], "far") for name in ("n1", "ctx", "n2", "act", "dqkv", "dh", "de", "ds")},
        {"keep": HALF, "give": HALF, "passed": (carried.shape, carried.dtype, "near")},
        {"f": scr((128 * CHUNK, 128), f32), "wide": scr(SQUARE, f32)},
    )


PIECES = 4


def merge_kernel(m):
    per = 64 // PIECES
    for piece in range(PIECES):
        m.need(f"keep_one{piece}", f"keep_two{piece}")
        keeps = m.__dict__[f"keep_one{piece}"], m.__dict__[f"keep_two{piece}"]

        def step(j, carry):
            chunk = pl.ds(pl.multiple_of((piece * per + j) * CHUNK, CHUNK), CHUNK)
            own = pl.ds(pl.multiple_of(j * CHUNK, CHUNK), CHUNK)
            for b, (kept, arrived) in enumerate(zip(keeps, (m.arrived_one, m.arrived_two))):
                total = kept[own, :].astype(f32) + arrived[chunk, :].astype(f32)
                to = pl.ds(pl.multiple_of((2 * j + b) * CHUNK, CHUNK), CHUNK)
                m.__dict__[f"both{piece}"][to, :] = total.astype(bf16)
            return carry

        lax.fori_loop(0, per, step, 0, unroll=4)
        m.ready(f"both{piece}")


def run_merge(keep_one, keep_two, arrived_one, arrived_two):
    ins = {"keep_two": keep_two, "keep_one": keep_one}
    near = {"arrived_one": arrived_one, "arrived_two": arrived_two}
    both = launch(
        merge_kernel,
        {name: (array, "parts") for name, array in ins.items()} | {name: (array, "near") for name, array in near.items()},
        {"both": ((128 * CHUNK, 128), bf16, "parts")},
    )["both"]
    return both.reshape(64, 2 * CHUNK, 128)


def finish_kernel(m):
    per = 64 // PIECES
    total = None
    for piece in range(PIECES):
        m.need(f"spread{piece}")
        part = m.__dict__[f"spread{piece}"]

        def step(i, carry):
            return carry + part[i].astype(f32)

        total = lax.fori_loop(0, per, step, total if piece else jnp.zeros((2 * CHUNK, 128), f32), unroll=2)
    m.total[...] = total
    for b in range(2):
        at = b * CHUNK
        for name, first, count, width in (("qkv", 0, 3, 9), ("proj", 27, 3, 3), ("expand", 36, 3, 12), ("contract", 72, 12, 3)):
            target = m.__dict__[f"{name}_{b}"]
            for r in range(count):
                for c in range(width):
                    row = at + first + r * width + c
                    target[r : r + 1, c * 128 : c * 128 + 128] = m.total[row : row + 1, :]


def lines_kernel(spread, lines_ref, near_ref, sems):
    copies = [
        pltpu.make_async_copy(spread.at[:, pl.ds(b * CHUNK + 96, 16), :], near_ref.at[b], sems.at[b]) for b in range(2)
    ]
    for copy in copies:
        copy.start()
    for b, copy in enumerate(copies):
        copy.wait()
        total = jnp.zeros((16, 128), f32)
        for i in range(64):
            total = total + near_ref[b, i].astype(f32)
        lines_ref[:, b, :] = jnp.broadcast_to(total[12:13], (128, 128))


def run_lines(spread):
    return pl.pallas_call(
        lines_kernel,
        out_shape=jax.ShapeDtypeStruct((128, 2, 128), f32),
        in_specs=[pl.BlockSpec(memory_space=pltpu.HBM)],
        out_specs=pl.BlockSpec(memory_space=pltpu.VMEM),
        scratch_shapes=[pltpu.VMEM((2, 64, 16, 128), bf16), pltpu.SemaphoreType.DMA((2,))],
        compiler_params=pltpu.CompilerParams(vmem_limit_bytes=VMEM_LIMIT),
    )(pltpu.with_memory_space_constraint(spread, pltpu.HBM))


def run_finish(spread):
    outs = {}
    for b in range(2):
        outs |= {f"qkv_{b}": ((3, 3 * D), f32, "near"), f"proj_{b}": ((3, D), f32, "near")}
        outs |= {f"expand_{b}": ((3, FF), f32, "near"), f"contract_{b}": ((12, D), f32, "near")}
    return launch(
        finish_kernel,
        {"spread": (spread, "parts")},
        outs,
        {"total": pltpu.VMEM((2 * CHUNK, 128), f32)},
    )


def passed_along(block, axis, distance):
    devices = range(lax.axis_size(axis))
    route = [((i - distance) % len(devices), i) for i in devices]
    return lax.ppermute(block, axis, route)


def edge_of(grid, dim, width, direction):
    extent = grid.shape[dim]
    if direction < 0:
        return lax.slice_in_dim(grid, 0, width, axis=dim)
    return lax.slice_in_dim(grid, extent - width, extent, axis=dim)


def rejoin(grid, dim, width, direction, arrived):
    extent = grid.shape[dim]
    if direction < 0:
        return jnp.concatenate([lax.slice_in_dim(grid, width, extent, axis=dim), arrived], axis=dim)
    return jnp.concatenate([arrived, lax.slice_in_dim(grid, 0, extent - width, axis=dim)], axis=dim)


def rolled_along(grid, dim, direction):
    width = (WT // 2, WH // 2, WW // 2)[dim]
    at = grid.ndim - 4 + dim
    moved = passed_along(edge_of(grid, at, width, direction), AXES[dim], direction)
    return rejoin(grid, at, width, direction, moved)


def rolled_twice(grid, direction):
    first = grid.ndim - 4
    sizes = [lax.axis_size(axis) for axis in AXES[:2]]
    parts = {}
    for bt in range(2):
        for bh in range(2):
            part = grid
            for at, width, moves in ((first, WT // 2, bt), (first + 1, WH // 2, bh)):
                extent = part.shape[at]
                if moves:
                    part = edge_of(part, at, width, direction)
                elif direction < 0:
                    part = lax.slice_in_dim(part, width, extent, axis=at)
                else:
                    part = lax.slice_in_dim(part, 0, extent - width, axis=at)
            if bt or bh:
                route = [
                    (t * sizes[1] + h, (t + bt * direction) % sizes[0] * sizes[1] + (h + bh * direction) % sizes[1])
                    for t in range(sizes[0])
                    for h in range(sizes[1])
                ]
                part = lax.ppermute(part, AXES[:2], route)
            parts[bt, bh] = part
    order = (0, 1) if direction < 0 else (1, 0)
    halves = [jnp.concatenate([parts[bt, bh] for bh in order], axis=first + 1) for bt in order]
    return jnp.concatenate(halves, axis=first)


def to_rows(grid):
    return jnp.pad(grid, ((0, 0), (0, 0), (0, 1), (0, 0))).reshape(ROWS, D)


def to_grid(flat):
    return flat.reshape(WT, WH, PITCH, D)[:, :, :WW]


def swapped(block):
    return lax.ppermute(block, "wa", [(i, i ^ 1) for i in range(lax.axis_size("wa"))])


def exchanged(both):
    groups = [[i for i in range(128) if i % 2 == side] for side in range(2)]
    return lax.all_to_all(both, AXES, 0, 0, axis_index_groups=groups, tiled=True)


def body(
    tokens, upstream, qkv_one, proj_one, table_one, expand_one, contract_one,
    qkv_two, proj_two, table_two, expand_two, contract_two,
):
    mine = (lax.axis_index("wa") % 2).astype(jnp.int32).reshape(1)
    x = to_rows(tokens)

    def far(wqkv, wp, we, wc):
        return {"wqkv": (wqkv, "far"), "wp": (wp, "far"), "we": (we, "far"), "wc": (wc, "far")}

    weights_one = far(qkv_one, proj_one, expand_one, contract_one)
    weights_two = far(qkv_two, proj_two, expand_two, contract_two)
    one = run_first_forward(x, table_one, weights_one)
    both = jnp.stack([to_grid(one["y"]), upstream])
    both = rolled_along(rolled_twice(both, -1), 2, -1)
    rolled, up = to_rows(both[0]), to_rows(both[1])
    two = run_second(rolled, up, table_two, {name: (w, "near") for name, (w, _) in weights_two.items()})
    gy = rolled_twice(to_grid(two["gy"]), 1)
    sent = passed_along(edge_of(gy, 2, WW // 2, 1), AXES[2], 1)
    sums_two = run_weights(mine, two, up, to_rows(gy))
    gy = to_rows(rejoin(to_grid(sums_two["passed"]), 2, WW // 2, 1, sent))
    arrived_two = swapped(sums_two["give"])
    sums_one = run_first_backward(mine, gy, x, one, weights_one)
    dx = sums_one["dx"]
    spread = exchanged(
        run_merge(sums_one["keep"], sums_two["keep"], swapped(sums_one["give"]), arrived_two)
    )
    tables = lax.all_to_all(run_lines(spread), AXES, 0, 0, tiled=True)
    done = run_finish(spread)

    def table_of(which):
        return tables[:120, which].reshape(HEADS, TPAD)[:, :TABLE]

    g1, g2 = ([done[f"{name}_{b}"] for name in ("qkv", "proj", "expand", "contract")] for b in range(2))
    return (
        to_grid(dx), g1[0], g1[1], table_of(0), g1[2], g1[3],
        g2[0], g2[1], table_of(1), g2[2], g2[3],
    )


def solution(mesh):
    grid = P("ta", "ha", "wa", None)
    rows_split = P(AXES, None)
    return jax.shard_map(
        body,
        mesh=mesh,
        in_specs=(grid, grid) + (P(),) * 10,
        out_specs=(
            grid, rows_split, rows_split, P(), rows_split, rows_split,
            rows_split, rows_split, P(), rows_split, rows_split,
        ),
        check_vma=False,
    )
```
